256 devices in a mesh: facet: 8 (over x_hi, y), sub: 32 (over z, x_lo, core).
Axes of the slice: x: 4 (x_hi: 2, x_lo: 2; x = x_hi * 2 + x_lo), y: 4, z: 8, core: 2. Of those that a mesh axis runs over, the one named last changes fastest.
Arguments:
- facets: float32 [8, 2, 64, 2048], P('facet', None, 'sub'), may hold values from -6 to 6
- taper_weight: float32 [2048], replicated, may hold values from 0.5 to 1.5
- offsets: int32 [256], replicated, may hold values from 0 to 65535
- point_coords: float32 [2, 1048576], P(None, ('facet', 'sub')), may hold values from -32 to 32
- owners: int32 [1048576, 1], P(('facet', 'sub')), may hold values from 0 to 31; in each aligned block of 4096 rows (0 to 4095, 4096 to 8191, ...) at most 512 rows name the same one
Outputs:
- visibilities: float32 [2, 1048576], P(None, ('facet', 'sub'))
The draws below stay inside these ranges and needn't reach their ends.
Inputs may be any that keep to these rules, and one draw needn't show every extreme that they name: `owners`: among the rows of one device no value is named by more than 512 rows, a bound that some block reaches.
All inputs are finite; a program needn't handle non-finite values.
Results may differ from the reference program's by a relative error of at most 0.0026.
Values may be sent and summed in bfloat16 or wider, within the bound.
No kernel may reach another device: no remote copies, remote signals or barrier semaphores. Data moves between devices by JAX's collectives and lax.ppermute only.
A program may use at most 128 MiB of HBM per device.

```python
import math
import jax
import jax.numpy as jnp
import numpy as np
from jax import lax

N_IMG = 65536
YB = 2048
XA = 256
VIS_DEV = 4096
FACETS = 8
SUBGRIDS = 256
R = 64
CAP = 512
VIS_ALL = 1048576
N_FACET = 8
N_SUB = 32


def place_ends(values, key, least, high):
    dims = values.shape
    index_at = [jax.random.randint(jax.random.fold_in(key, axis), (), 0, dims[axis]) for axis in range(len(dims))]
    values = values.at[tuple(index_at)].set(least)
    longest = dims.index(max(dims))
    index_at[longest] = (index_at[longest] + 1) % dims[longest]
    return values.at[tuple(index_at)].set(high)


def levels(own_key, shape, cuts, low, high):
    loudness, own = 1.0, jax.random.fold_in(own_key, 6)
    for dim, shards_of in cuts:
        heights = jnp.exp(jax.random.uniform(jax.random.fold_in(own, dim), (shards_of,), jnp.float32, low / len(cuts), high / len(cuts)))
        loudness = loudness * jnp.repeat(heights, shape[dim] // shards_of).reshape([-1 if axis == dim else 1 for axis in range(len(shape))])
    return loudness


def deal_out(rng, own, number, rows, number_of, top, bound, slope):
    order = jax.random.permutation(rng, number_of)
    packed, usual = shares(number_of, rows * top, bound, slope, True), shares(number_of, rows * top, bound, slope, False)
    places = jnp.arange(number_of)

    def named(sizes, offset_by):
        used = int((sizes > 0).sum())
        fixed = max(1, used // 4)
        moved = fixed + (places - fixed + offset_by * (used - fixed)) % max(1, number_of - fixed)
        return jnp.zeros((number_of,), jnp.int32).at[order[jnp.where(places < fixed, places, moved)]].set(jnp.asarray(sizes, jnp.int32))

    sizes = jnp.where(number % 4 == 0, named(packed, number // 4), named(usual, number - number // 4 - 1))
    mixed = jax.random.permutation(jax.random.fold_in(own, 3), number_of)
    source_of, taker = mixed[0:number_of // 2 * 2:2], mixed[1:number_of // 2 * 2:2]
    margin = jnp.minimum(sizes[source_of] - 1, bound - sizes[taker]) // 2
    margin = jnp.where((source_of == order[0]) | (taker == order[0]) | (sizes[taker] == 0), 0, jnp.maximum(margin, 0))
    moved = jax.random.randint(jax.random.fold_in(own, 4), (number_of // 2,), 0, 1 << 20) % (margin + 1)
    sizes = sizes.at[source_of].add(-moved).at[taker].add(moved)
    items = jnp.searchsorted(jnp.cumsum(sizes), jnp.arange(rows * top), side="right").astype(jnp.int32)
    listing = items.reshape(top, rows).T
    listing = listing[jax.random.permutation(jax.random.fold_in(own, 1), rows)]
    offset_by = jax.random.randint(jax.random.fold_in(own, 2), (rows, 1), 0, top)
    return jnp.take_along_axis(listing, (jnp.arange(top)[None, :] + offset_by) % top, axis=1)


def shares(number_of, total, reach, lean, full):
    weights = [(1 << 20) // math.isqrt(grade ** lean) + 1 for grade in range(1, number_of + 1)]
    largest = reach if full else min(reach, max(-(-total // number_of), total * weights[0] // sum(weights)))
    least = 1 if total - largest >= number_of - 1 else 0
    given, rest = [largest] + [least] * (number_of - 1), total - largest - least * (number_of - 1)
    while rest > 0:
        candidates = [i for i in range(1, number_of) if given[i] < largest] or [i for i in range(1, number_of) if given[i] < reach]
        mass, left = sum([weights[i] for i in candidates]), rest
        for i in candidates:
            addition = min(reach - given[i], max(1, left * weights[i] // mass), rest)
            given[i] = given[i] + addition
            rest = rest - addition
    return np.array(given)


def noise(key, shape, deviation, most, pieces=(), kind=jnp.bfloat16):
    array = jax.random.normal(key, shape, jnp.float32) * deviation
    if len(pieces) > 0:
        array = levels(key, shape, pieces, -0.22, 0.18) * array
    return jnp.clip(array, min=-most, max=most).astype(kind)


def setup_inputs(seed: int = 0) -> dict:
    streams_of = jax.random.split(jax.random.key(seed), 6)
    facets = noise(streams_of[0], (FACETS, 2, R, YB), 1.0, 6.0, ((0, 8), (2, 32)), jnp.float32)
    taper_weight = jnp.clip(jax.random.uniform(streams_of[1], (YB,), jnp.float32, 0.5, 1.5), 0.5, 1.5)
    offsets = place_ends(jax.random.randint(streams_of[2], (SUBGRIDS,), 0, N_IMG), jax.random.fold_in(streams_of[2], 1), 0, N_IMG - 1).astype(jnp.int32)
    point_coords = jnp.clip(jax.random.uniform(streams_of[3], (2, VIS_ALL), jnp.float32, -32.0, 32.0) * levels(streams_of[3], (2, VIS_ALL), ((1, 256),), -0.4, 0.0), -32.0, 32.0)
    owners_keys = jax.random.split(jax.random.fold_in(streams_of[4], 1), VIS_ALL // VIS_DEV)
    owners_turns = jax.random.permutation(jax.random.fold_in(streams_of[4], 3), VIS_ALL // VIS_DEV)
    owners = jax.vmap(lambda own, number: deal_out(jax.random.fold_in(streams_of[4], 2), own, number, VIS_DEV, N_SUB, 1, CAP, 2))(owners_keys, owners_turns).reshape((VIS_ALL, 1))
    return {"facets": facets, "taper_weight": taper_weight, "offsets": offsets, "point_coords": point_coords, "owners": owners}


TWO_PI = 2.0 * math.pi

def product_mod(first, second):
    first = first % N_IMG
    second = second % N_IMG
    return (first * (second // 256) % N_IMG * 256 + first * (second % 256)) % N_IMG

def unit_phase(index):
    angle_rad = index.astype(jnp.float32) * (TWO_PI / N_IMG)
    return (jnp.cos(angle_rad), -jnp.sin(angle_rad))

def transform_table(facet_width, cell_count):
    columns = jnp.arange(facet_width, dtype=jnp.int32)
    cell_index = jnp.arange(cell_count, dtype=jnp.int32)
    table_real, table_imag = unit_phase(product_mod(columns[:, None], cell_index[None, :]))
    upper = jnp.concatenate([table_real, table_imag], axis=1)
    lower = jnp.concatenate([-table_imag, table_real], axis=1)
    return jnp.concatenate([upper, lower], axis=0)

def contributions(facet_image, facet_index, offset_part, taper_weight, transform, norm_factor):
    facet_width = facet_image.shape[2]
    row_count = facet_image.shape[1]
    cell_count = transform.shape[1] // 2
    sub_total = offset_part.shape[0]
    columns = jnp.arange(facet_width, dtype=jnp.int32)
    offset_real, offset_imag = unit_phase(product_mod(offset_part[:, None], columns[None, :]))
    image_real = facet_image[0] * taper_weight
    image_imag = facet_image[1] * taper_weight
    shifted_real = image_real[None] * offset_real[:, None] - image_imag[None] * offset_imag[:, None]
    shifted_imag = image_real[None] * offset_imag[:, None] + image_imag[None] * offset_real[:, None]
    stacked = jnp.concatenate([shifted_real, shifted_imag], axis=2).reshape(sub_total * row_count, 2 * facet_width)
    product = jnp.dot(stacked, transform, precision=lax.Precision.HIGHEST, preferred_element_type=jnp.float32)
    product = product.reshape(sub_total, row_count, 2 * cell_count)
    product_real = product[..., :cell_count]
    product_imag = product[..., cell_count:]
    anchor = facet_index * facet_width
    cell_index = jnp.arange(cell_count, dtype=jnp.int32)
    twist_index = (product_mod(offset_part, anchor)[:, None] + product_mod(cell_index, anchor)[None, :]) % N_IMG
    twist_real, twist_imag = unit_phase(twist_index)
    result_real = (product_real * twist_real[:, None] - product_imag * twist_imag[:, None]) * norm_factor
    result_imag = (product_real * twist_imag[:, None] + product_imag * twist_real[:, None]) * norm_factor
    return jnp.stack([result_real, result_imag], axis=1)

def centered(cell_count):
    return (jnp.arange(cell_count, dtype=jnp.float32) - cell_count // 2) / cell_count

def phase_pair(scaled, position):
    angle_rad = TWO_PI * scaled * position
    return (jnp.cos(angle_rad), jnp.sin(angle_rad))

def to_bfloat(values):
    return lax.optimization_barrier(values.astype(jnp.bfloat16)).astype(jnp.float32)

def reference(facets, taper_weight, offsets, point_coords, owners):
    transform = transform_table(YB, XA)
    norm_factor = 1.0 / math.sqrt(FACETS * YB)
    groups = offsets.reshape(N_FACET, N_SUB)

    def add_facet(running, member):
        facet_image, facet_index = member
        part_sums = lax.map(lambda offset_part: contributions(facet_image, facet_index, offset_part, taper_weight, transform, norm_factor), groups)
        return (running + part_sums, None)
    zero_sums = jnp.zeros((N_FACET, N_SUB, 2, R, XA), jnp.float32)
    running, _ = lax.scan(add_facet, zero_sums, (facets, jnp.arange(FACETS, dtype=jnp.int32)))
    subgrid = running.reshape(SUBGRIDS, 2, R, XA).astype(jnp.bfloat16)
    total_rows = point_coords.shape[1]
    piece_rows = math.gcd(VIS_DEV, 256)
    row_index = jnp.arange(total_rows, dtype=jnp.int32)
    target = row_index // VIS_DEV // N_SUB * N_SUB + owners[:, 0]
    point_pieces = point_coords.reshape(2, total_rows // piece_rows, piece_rows).transpose(1, 0, 2)
    target_pieces = target.reshape(total_rows // piece_rows, piece_rows)
    col_position = centered(XA)
    row_position = centered(R)
    vis_scale = 1.0 / math.sqrt(R * XA)

    def one_piece(member):
        points, chosen = member
        picked = subgrid[chosen].astype(jnp.float32)
        grid_real = picked[:, 0]
        grid_imag = picked[:, 1]
        col_real, col_imag = phase_pair(points[1][:, None], col_position[None, :])
        col_real = to_bfloat(col_real)
        col_imag = to_bfloat(col_imag)
        highest = lax.Precision.HIGHEST
        inner_real = jnp.einsum('nab,nb->na', grid_real, col_real, precision=highest) - jnp.einsum('nab,nb->na', grid_imag, col_imag, precision=highest)
        inner_imag = jnp.einsum('nab,nb->na', grid_real, col_imag, precision=highest) + jnp.einsum('nab,nb->na', grid_imag, col_real, precision=highest)
        row_real, row_imag = phase_pair(points[0][:, None], row_position[None, :])
        value_real = lax.optimization_barrier(jnp.sum(row_real * inner_real - row_imag * inner_imag, axis=1)) * vis_scale
        value_imag = lax.optimization_barrier(jnp.sum(row_real * inner_imag + row_imag * inner_real, axis=1)) * vis_scale
        return jnp.stack([value_real, value_imag])
    by_piece = lax.map(one_piece, (point_pieces, target_pieces))
    return by_piece.transpose(1, 0, 2).reshape(2, total_rows)
```

```python
import math

import jax
import jax.numpy as jnp
import ml_dtypes
import numpy as np
from jax import lax
from jax.experimental import pallas as pl
from jax.experimental.pallas import tpu as pltpu
from jax.sharding import PartitionSpec as P

N_IMG = 65536
XA = 256
ROWS = 64
SUBS = 32
CAP = 512
DEV_ROWS = 4096
F32 = jnp.float32
BF16 = jnp.bfloat16


def split_host(table):
    table = np.asarray(table, np.float32)
    high = table.astype(ml_dtypes.bfloat16)
    low = (table - high.astype(np.float32)).astype(ml_dtypes.bfloat16)
    return high, low


def transform_tables():
    turn = 2.0 * np.pi / 256.0
    a, q = np.arange(64), np.arange(256)
    first = np.outer(a, q) % 256 * turn
    real, imag = np.cos(first), -np.sin(first)
    outer = np.block([[real, imag], [-imag, real]])
    angle = np.outer(q, q) * (2.0 * np.pi / N_IMG)
    twiddle = np.stack([np.cos(angle), -np.sin(angle)]) / 128.0
    second = np.outer(q, q) % 256 * turn
    real, imag = np.cos(second), -np.sin(second)
    inner = np.block([[real, -imag], [imag, real]])
    return split_host(outer) + (twiddle.astype(np.float32),) + split_host(inner)


def fold_tables():
    order = []
    for h in range(8):
        order += [16 * h + 8 - l for l in range(8)] + [16 * h + 9 + l for l in range(8)]
    cells = np.zeros((XA, 2 * 128), np.float32)
    for place, m in enumerate(order):
        if m < 128:
            cells[128 + m, place] += 1.0
            cells[128 + m, 128 + place] += 1.0
        cells[128 - m, place] += 1.0
        cells[128 - m, 128 + place] -= 1.0
    order = []
    for h in range(2):
        order += [16 * h + 7 - l for l in range(8)] + [16 * h + 8 + l for l in range(8)]
    rows = np.zeros((ROWS, ROWS), np.float32)
    for place, k in enumerate(order):
        upper, lower = 32 + k, 31 - k
        upper_at = upper % 2 * SUBS + upper // 2
        lower_at = lower % 2 * SUBS + lower // 2
        rows[place, upper_at] = rows[place, lower_at] = 1.0
        rows[32 + place, upper_at], rows[32 + place, lower_at] = 1.0, -1.0
    return cells.astype(ml_dtypes.bfloat16), rows


def turn_polynomials():
    nodes = (np.cos(np.pi * (np.arange(400) + 0.5) / 400) + 1.0) / 8.0
    r = np.sqrt(nodes)
    fit = np.polynomial.chebyshev.Chebyshev.fit
    cosine = fit(nodes, np.cos(2 * np.pi * r), 7, domain=[0, 0.25])
    sine = fit(nodes, np.sin(2 * np.pi * r) / r, 6, domain=[0, 0.25])
    plain = np.polynomial.Polynomial
    return (
        [float(c) for c in cosine.convert(kind=plain).coef],
        [float(c) for c in sine.convert(kind=plain).coef],
    )


COS_TERMS, SIN_TERMS = turn_polynomials()


def unit_turns(turns):
    r = turns - jnp.round(turns)
    square = r * r
    cosine = jnp.full_like(square, COS_TERMS[-1])
    for term in COS_TERMS[-2::-1]:
        cosine = cosine * square + term
    sine = jnp.full_like(square, SIN_TERMS[-1])
    for term in SIN_TERMS[-2::-1]:
        sine = sine * square + term
    return cosine, sine * r


def pieces_of(values):
    first = values.astype(BF16)
    rest = values - first.astype(F32)
    second = rest.astype(BF16)
    third = (rest - second.astype(F32)).astype(BF16)
    return first, second, third


def iota(shape, axis):
    return lax.broadcasted_iota(jnp.int32, shape, axis)


def pack_kernel(coords_ref, owners_ref, packed_ref, position_ref):
    width = 256
    owner_of = iota((SUBS, width), 0)
    slot_of = iota((CAP, width), 0)
    upper = (iota((width, width), 0) <= iota((width, width), 1)).astype(BF16)
    carry = jnp.zeros((SUBS, 1), F32)
    total = jnp.zeros((6 * SUBS, CAP), F32)
    for block in range(DEV_ROWS // width):
        lanes = pl.ds(block * width, width)
        match = owners_ref[:, lanes] == owner_of
        hot = match.astype(F32)
        running = jnp.dot(hot.astype(BF16), upper, preferred_element_type=F32) + carry
        rank = jnp.sum(hot * running, axis=0, keepdims=True) - 1.0
        carry = carry + jnp.sum(hot, axis=1, keepdims=True)
        position = rank.astype(jnp.int32)
        position_ref[:, lanes] = position
        slots = (slot_of == position).astype(F32).astype(BF16)
        rows = []
        for axis in range(2):
            for piece in pieces_of(coords_ref[axis : axis + 1, lanes]):
                rows.append((hot * piece.astype(F32)).astype(BF16))
        total = total + lax.dot_general(
            jnp.concatenate(rows, axis=0),
            slots,
            (((1,), (1,)), ((), ())),
            preferred_element_type=F32,
        )
    for axis in range(2):
        at = 96 * axis
        values = total[at : at + 32] + (total[at + 32 : at + 64] + total[at + 64 : at + 96])
        packed_ref[:, 2 * axis, :] = values[:, :256]
        packed_ref[:, 2 * axis + 1, :] = values[:, 256:]


def split_dot(left_pair, right_pair):
    left_high, left_low = left_pair
    right_high, right_low = right_pair
    out = jnp.dot(left_high, right_high, preferred_element_type=F32)
    out = out + jnp.dot(left_low, right_high, preferred_element_type=F32)
    return out + jnp.dot(left_high, right_low, preferred_element_type=F32)


def split_in_kernel(values):
    high = values.astype(BF16)
    return high, (values - high.astype(F32)).astype(BF16)


def window_kernel(
    starts_ref, image_ref, packed_ref, outer_h, outer_l, twiddle_ref, inner_h, inner_l, out_ref, spectrum
):
    planes = []
    for r in range(2):
        stacked = jnp.concatenate(
            [image_ref[f, 2 * part + r] for part in range(2) for f in range(8)], axis=0
        )
        mixed = split_dot(split_in_kernel(stacked.T), (outer_h[...], outer_l[...]))
        real, imag = mixed[:, :256], mixed[:, 256:]
        turn_real, turn_imag = twiddle_ref[0], twiddle_ref[1]
        planes.append(
            jnp.concatenate(
                [real * turn_real - imag * turn_imag, real * turn_imag + imag * turn_real], axis=0
            )
        )
    for r in range(2):
        result = split_dot((inner_h[...], inner_l[...]), split_in_kernel(planes[r]))
        spectrum[:, r, :] = result[:256]
        spectrum[:, 2 + r, :] = result[256:]
    lane = iota((4, 256), 1)
    for s in range(SUBS):
        start = starts_ref[s]
        high = start // 256
        low = start % 256
        here = spectrum[high]
        following = spectrum[(high + 1) % 256]
        window = jnp.where(lane >= low, here, following)
        window = pltpu.roll(window, (256 - low) % 256, 1)
        window = window.astype(BF16).astype(F32)
        out_ref[s] = jnp.concatenate([window, packed_ref[s]], axis=0)


def degrid_kernel(arrived_ref, cells_ref, rows_ref, out_ref, weights, bias, phases):
    exact = lax.Precision.HIGHEST
    folded = []
    constant = []
    for part in range(2):
        grid = jnp.concatenate(
            [arrived_ref[:, 2 * part, :], arrived_ref[:, 2 * part + 1, :]], axis=0
        )
        by_cell = jnp.dot(grid.astype(BF16), cells_ref[...], preferred_element_type=F32)
        folded.append(jnp.dot(rows_ref[...], by_cell, precision=exact, preferred_element_type=F32))
        middle = jnp.dot(rows_ref[...], grid, precision=exact, preferred_element_type=F32)
        constant.append(middle[:, 128:129])
    (real, imag), (real_mid, imag_mid) = folded, constant
    even, odd = slice(0, 32), slice(32, 64)
    cosine, sine = slice(0, 128), slice(128, 256)
    groups = (
        (real[even, cosine], -imag[even, sine], real_mid[even]),
        (imag[odd, cosine], real[odd, sine], imag_mid[odd]),
        (imag[even, cosine], real[even, sine], imag_mid[even]),
        (real[odd, cosine], -imag[odd, sine], real_mid[odd]),
    )
    for number, (left, right, middle) in enumerate(groups):
        at = pl.ds(32 * number, 32)
        weights[at, :] = jnp.concatenate([left, right], axis=1).astype(BF16)
        bias[at, :] = jnp.broadcast_to(middle, (32, 256))

    step = iota((8, 256), 0).astype(F32)
    centre_scale = (16.0 * step + 8.5) * (1.0 / XA)
    offset_scale = (step + 0.5) * (1.0 / XA)
    row_scale = (step + 0.5) * (1.0 / ROWS)

    def chunk(source, half):
        v = arrived_ref[source, 4 + half : 5 + half, :]
        u = arrived_ref[source, 6 + half : 7 + half, :]
        centre_cos, centre_sin = unit_turns(u * centre_scale)
        offset_cos, offset_sin = unit_turns(u * offset_scale)
        row_cos, row_sin = unit_turns(v * row_scale)
        for h in range(8):
            a_cos, a_sin = centre_cos[h : h + 1], centre_sin[h : h + 1]
            cc, ss = a_cos * offset_cos, a_sin * offset_sin
            sc, cs = a_sin * offset_cos, a_cos * offset_sin
            at = 16 * h
            phases[half, at : at + 16, :] = jnp.concatenate([cc + ss, cc - ss], axis=0).astype(BF16)
            phases[half, 128 + at : 144 + at, :] = jnp.concatenate(
                [sc - cs, sc + cs], axis=0
            ).astype(BF16)
        inner = jnp.dot(weights[...], phases[half], preferred_element_type=F32) + bias[...]
        first_cos, first_sin = row_cos[0:1], row_sin[0:1]
        last_cos, last_sin = row_cos[7:8], row_sin[7:8]
        eight_cos = first_cos * last_cos - first_sin * last_sin
        eight_sin = first_cos * last_sin + first_sin * last_cos
        two_cos = eight_cos * eight_cos - eight_sin * eight_sin
        two_sin = 2.0 * eight_cos * eight_sin
        three_cos = eight_cos * two_cos - eight_sin * two_sin
        three_sin = eight_cos * two_sin + eight_sin * two_cos
        total_real = jnp.zeros((8, 256), F32)
        total_imag = jnp.zeros((8, 256), F32)
        for h, (a_cos, a_sin) in enumerate(((eight_cos, eight_sin), (three_cos, three_sin))):
            cc, ss = a_cos * row_cos, a_sin * row_sin
            sc, cs = a_sin * row_cos, a_cos * row_sin
            for side, (cosk, sink) in enumerate(((cc + ss, sc - cs), (cc - ss, sc + cs))):
                at = 16 * h + 8 * side
                total_real += inner[at : at + 8] * cosk - inner[32 + at : 40 + at] * sink
                total_imag += inner[64 + at : 72 + at] * cosk + inner[96 + at : 104 + at] * sink
        real_sum = jnp.sum(total_real, axis=0, keepdims=True) * (1.0 / 128.0)
        imag_sum = jnp.sum(total_imag, axis=0, keepdims=True) * (1.0 / 128.0)
        out_ref[source, half : half + 1, :] = real_sum * first_cos + imag_sum * first_sin
        out_ref[source, 2 + half : 3 + half, :] = imag_sum * first_cos - real_sum * first_sin

    def both(source, carry):
        chunk(source, 0)
        chunk(source, 1)
        return carry

    lax.fori_loop(0, SUBS, both, 0)


def unpack_kernel(returned_ref, owners_ref, position_ref, out_ref):
    rows = []
    for axis in range(2):
        values = jnp.concatenate(
            [returned_ref[:, 2 * axis, :], returned_ref[:, 2 * axis + 1, :]], axis=1
        )
        rows += list(pieces_of(values))
    table = jnp.concatenate(rows, axis=0)
    width = 512
    owner_of = iota((SUBS, width), 0)
    slot_of = iota((CAP, width), 0)
    for block in range(DEV_ROWS // width):
        lanes = pl.ds(block * width, width)
        match = owners_ref[:, lanes] == owner_of
        slots = (slot_of == position_ref[:, lanes]).astype(F32).astype(BF16)
        picked = jnp.dot(table, slots, preferred_element_type=F32)
        for axis in range(2):
            at = 96 * axis
            values = picked[at : at + 32] + (picked[at + 32 : at + 64] + picked[at + 64 : at + 96])
            out_ref[axis : axis + 1, lanes] = jnp.sum(
                jnp.where(match, values, 0.0), axis=0, keepdims=True
            )


def vmem():
    return pl.BlockSpec(memory_space=pltpu.VMEM)


def call(kernel, out_shape, in_specs, scratch, flops, *operands):
    return pl.pallas_call(
        kernel,
        out_shape=out_shape,
        in_specs=in_specs,
        out_specs=jax.tree.map(lambda _: vmem(), out_shape),
        scratch_shapes=scratch,
        compiler_params=pltpu.CompilerParams(vmem_limit_bytes=40 * 1024 * 1024),
        cost_estimate=pl.CostEstimate(flops=flops, bytes_accessed=1 << 20, transcendentals=0),
    )(*operands)


def per_device(facets, taper_weight, offsets, point_coords, owners):
    facet_index = lax.axis_index("facet")
    image = (facets[0] * taper_weight).reshape(4, 8, 256)
    image = lax.all_to_all(
        jnp.broadcast_to(image[None], (8, 4, 8, 256)), "facet", split_axis=0, concat_axis=0, tiled=True
    )
    owner_row = owners.reshape(1, DEV_ROWS)
    packed, position = call(
        pack_kernel,
        (
            jax.ShapeDtypeStruct((SUBS, 4, 256), F32),
            jax.ShapeDtypeStruct((1, DEV_ROWS), jnp.int32),
        ),
        [vmem()] * 2,
        [],
        1 << 32,
        point_coords,
        owner_row,
    )
    starts = lax.dynamic_slice(offsets, (facet_index * SUBS,), (SUBS,))
    outer_h, outer_l, twiddle, inner_h, inner_l = transform_tables()
    payload = call(
        window_kernel,
        jax.ShapeDtypeStruct((SUBS, 8, 256), F32),
        [pl.BlockSpec(memory_space=pltpu.SMEM)] + [vmem()] * 7,
        [pltpu.VMEM((256, 4, 256), F32)],
        1 << 32,
        starts,
        image,
        packed,
        outer_h,
        outer_l,
        twiddle,
        inner_h,
        inner_l,
    )
    arrived = lax.all_to_all(payload, "sub", split_axis=0, concat_axis=0, tiled=True)
    cells, rows = fold_tables()
    values = call(
        degrid_kernel,
        jax.ShapeDtypeStruct((SUBS, 4, 256), F32),
        [vmem()] * 3,
        [
            pltpu.VMEM((128, 256), BF16),
            pltpu.VMEM((128, 256), F32),
            pltpu.VMEM((2, 256, 256), BF16),
        ],
        1 << 32,
        arrived,
        cells,
        rows,
    )
    returned = lax.all_to_all(values, "sub", split_axis=0, concat_axis=0, tiled=True)
    return call(
        unpack_kernel,
        jax.ShapeDtypeStruct((2, DEV_ROWS), F32),
        [vmem()] * 3,
        [],
        1 << 32,
        returned,
        owner_row,
        position,
    )


def solution(mesh):
    placed = (
        P("facet", None, "sub", None),
        P(),
        P(),
        P(None, ("facet", "sub")),
        P(("facet", "sub"), None),
    )
    return jax.shard_map(
        per_device, mesh=mesh, in_specs=placed, out_specs=P(None, ("facet", "sub")), check_vma=False
    )
```

```python
import math

import jax
import jax.numpy as jnp
import ml_dtypes
import numpy as np
from jax import lax
from jax.experimental import pallas as pl
from jax.experimental.pallas import tpu as pltpu
from jax.sharding import PartitionSpec as P

N_IMG = 65536
XA = 256
ROWS = 64
SUBS = 32
CAP = 512
DEV_ROWS = 4096
PARTS = 4
F32 = jnp.float32
BF16 = jnp.bfloat16


def split_host(table):
    table = np.asarray(table, np.float32)
    high = table.astype(ml_dtypes.bfloat16)
    low = (table - high.astype(np.float32)).astype(ml_dtypes.bfloat16)
    return high, low


def transform_tables():
    turn = 2.0 * np.pi / 256.0
    a, q = np.arange(64), np.arange(256)
    first = np.outer(a, q) % 256 * turn
    real, imag = np.cos(first), -np.sin(first)
    outer = np.block([[real, imag], [-imag, real]])
    angle = np.outer(q, q) * (2.0 * np.pi / N_IMG)
    twiddle = np.stack([np.cos(angle), -np.sin(angle)]) / 128.0
    second = np.outer(q, q) % 256 * turn
    real, imag = np.cos(second), -np.sin(second)
    inner = np.block([[real, -imag], [imag, real]])
    return split_host(outer) + (twiddle.astype(np.float32),) + split_host(inner)


def fold_tables():
    order = [16 * h + 1 + j for j in range(16) for h in range(8)]
    cells = np.zeros((XA, 3 * 128), np.float32)
    for place, m in enumerate(order):
        if m < 128:
            cells[128 + m, place] += 1.0
            cells[128 + m, 128 + place] += 1.0
        cells[128 - m, place] += 1.0
        cells[128 - m, 128 + place] -= 1.0
    cells[128, 256:] = 1.0
    order = [4 * g + j for j in range(4) for g in range(8)]
    even, odd = np.zeros((2, 32, ROWS), np.float32)
    for place, k in enumerate(order):
        for row, sign in ((32 + k, 1.0), (31 - k, -1.0)):
            at = row % 2 * SUBS + row // 2
            even[place, at], odd[place, at] = 1.0, sign
    none = np.zeros_like(even)
    with_cos = np.block([[even, none], [none, odd], [none, even], [odd, none]])
    with_sin = np.block([[none, -even], [odd, none], [even, none], [none, -odd]])
    return [table.astype(ml_dtypes.bfloat16) for table in (cells, with_cos, with_sin)]


def turn_polynomials(reach, cos_terms, sin_terms):
    nodes = (np.cos(np.pi * (np.arange(400) + 0.5) / 400) + 1.0) / 2.0 * reach**2
    r = np.sqrt(nodes)
    fit = np.polynomial.chebyshev.Chebyshev.fit
    cosine = fit(nodes, np.cos(2 * np.pi * r), cos_terms - 1, domain=[0, reach**2])
    sine = fit(nodes, np.sin(2 * np.pi * r) / r, sin_terms - 1, domain=[0, reach**2])
    plain = np.polynomial.Polynomial
    return (
        [float(c) for c in cosine.convert(kind=plain).coef],
        [float(c) for c in sine.convert(kind=plain).coef],
    )


ANY_TURN = turn_polynomials(0.5, 7, 6)
QUARTER_TURN = turn_polynomials(0.25, 5, 5)
SMALL_TURN = turn_polynomials(0.0625, 4, 3)


def reduced(turns):
    return turns - jnp.round(turns)


def unit_turns(r, terms):
    square = r * r
    cosine, sine = (jnp.full_like(square, part[-1]) for part in terms)
    for term in terms[0][-2::-1]:
        cosine = cosine * square + term
    for term in terms[1][-2::-1]:
        sine = sine * square + term
    return cosine, sine * r


def double_cos(half_step):
    return 2.0 - 4.0 * (half_step[1] * half_step[1])


def step_on(last, before, twice):
    return tuple(twice * x - y for x, y in zip(last, before))


def split_in_kernel(values):
    high = values.astype(BF16)
    return high, (values - high.astype(F32)).astype(BF16)


def iota(shape, axis):
    return lax.broadcasted_iota(jnp.int32, shape, axis)


def pack_kernel(coords_ref, owners_ref, packed_ref, position_ref):
    width = 256
    blocks = DEV_ROWS // width
    owner_of = iota((SUBS, width), 0)
    slot_of = iota((CAP, width), 0)
    upper = (iota((width, width), 0) <= iota((width, width), 1)).astype(F32).astype(BF16)
    hots = []
    for block in range(blocks):
        match = owners_ref[:, pl.ds(block * width, width)] == owner_of
        hots.append(match.astype(F32))
    running = jnp.dot(
        jnp.concatenate(hots, axis=0).astype(BF16), upper, preferred_element_type=F32
    )
    carry = jnp.zeros((SUBS, 1), F32)
    positions = []
    for block in range(blocks):
        mine = running[SUBS * block : SUBS * block + SUBS]
        rank = jnp.sum(hots[block] * (mine + carry), axis=0, keepdims=True) - 1.0
        carry = carry + mine[:, width - 1 : width]
        positions.append(rank.astype(jnp.int32))
        position_ref[:, pl.ds(block * width, width)] = positions[-1]
    total = jnp.zeros((4 * SUBS, CAP), F32)
    for block in range(blocks):
        lanes = pl.ds(block * width, width)
        slots = (slot_of == positions[block]).astype(F32).astype(BF16)
        rows = []
        for axis in range(2):
            for piece in split_in_kernel(coords_ref[axis : axis + 1, lanes]):
                rows.append((hots[block] * piece.astype(F32)).astype(BF16))
        total = total + lax.dot_general(
            jnp.concatenate(rows, axis=0),
            slots,
            (((1,), (1,)), ((), ())),
            preferred_element_type=F32,
        )
    for piece in range(4):
        for quarter in range(4):
            packed_ref[:, 4 * piece + quarter, :] = total[
                SUBS * piece : SUBS * piece + SUBS, 128 * quarter : 128 * quarter + 128
            ]


def split_dot(left_pair, right_pair):
    left_high, left_low = left_pair
    right_high, right_low = right_pair
    out = jnp.dot(left_high, right_high, preferred_element_type=F32)
    out = out + jnp.dot(left_low, right_high, preferred_element_type=F32)
    return out + jnp.dot(left_high, right_low, preferred_element_type=F32)


def spread_kernel(facets_ref, out_ref, rows):
    for part in range(2):
        for r in range(2):
            for block in range(16):
                at = 32 * part + 16 * r + block
                rows[at : at + 1, :] = facets_ref[
                    0, part, r : r + 1, 128 * block : 128 * block + 128
                ]
    for f in range(8):
        out_ref[f] = rows[...]


def window_kernel(
    starts_ref,
    image_ref,
    taper_ref,
    packed_ref,
    outer_h,
    outer_l,
    twiddle_ref,
    inner_h,
    inner_l,
    out_ref,
    columns,
    spectrum,
    payload,
):
    planes = []
    for r in range(2):
        for part in range(2):
            for f in range(8):
                for side in range(2):
                    line = image_ref[f, pl.ds(32 * part + 16 * r + side, 8, stride=2), :]
                    at = 64 * part + 8 * f
                    columns[r, at : at + 8, 128 * side : 128 * side + 128] = (
                        line * taper_ref[pl.ds(side, 8, stride=2), :]
                    )
        mixed = split_dot(split_in_kernel(columns[r].T), (outer_h[...], outer_l[...]))
        real, imag = mixed[:, :256], mixed[:, 256:]
        turn_real, turn_imag = twiddle_ref[0], twiddle_ref[1]
        planes.append(
            jnp.concatenate(
                [real * turn_real - imag * turn_imag, real * turn_imag + imag * turn_real], axis=0
            )
        )
    for r in range(2):
        result = split_dot((inner_h[...], inner_l[...]), split_in_kernel(planes[r]))
        spectrum[:, r, :] = result[:256]
        spectrum[:, 2 + r, :] = result[256:]
    lane = iota((4, 256), 1)
    for s in range(SUBS):
        start = starts_ref[s]
        high = start // 256
        low = start % 256
        here = spectrum[high]
        following = spectrum[(high + 1) % 256]
        window = jnp.where(lane >= low, here, following)
        window = pltpu.roll(window, (256 - low) % 256, 1)
        payload[s] = jnp.concatenate([window[:, :128], window[:, 128:], packed_ref[s]], axis=0)
    out_ref[...] = payload[...].astype(BF16)


def degrid_kernel(
    arrived_ref, cells_ref, with_cos_ref, with_sin_ref, out_ref, arrived, coords, weights, bias, partial, values, *buffers
):
    arrived[...] = arrived_ref[...].astype(F32)
    grid = jnp.concatenate(
        [
            jnp.concatenate([arrived[:, 4 * side + plane, :] for plane in range(4)], axis=0)
            for side in range(2)
        ],
        axis=1,
    )
    for axis in range(2):
        for quarter in range(4):
            at = 8 + 8 * axis + quarter
            coords[axis, quarter] = arrived[:, at, :] + arrived[:, at + 4, :]
    by_cell = jnp.dot(grid.astype(BF16), cells_ref[...], preferred_element_type=F32)
    high, low = split_in_kernel(by_cell)

    def fold(matrix, columns):
        return jnp.dot(matrix, high[:, columns], preferred_element_type=F32) + jnp.dot(
            matrix, low[:, columns], preferred_element_type=F32
        )

    weights[:, 0:128] = fold(with_cos_ref[...], slice(0, 128)).astype(BF16)
    weights[:, 128:256] = fold(with_sin_ref[...], slice(128, 256)).astype(BF16)
    bias[...] = fold(with_cos_ref[...], slice(256, 384))

    step_row = iota((8, 256), 0).astype(F32)
    cell_scale = (16.0 * step_row + 8.5) * (1.0 / XA)
    row_scale = (4.0 * step_row + 2.0) * (1.0 / ROWS)
    def place(step, part):
        return (step * PARTS + part) // 2, part % 2

    def beside(step, part, axis):
        source, half = place(step, part)
        where = jnp.concatenate(
            [
                jnp.broadcast_to(
                    coords[1 - axis, 2 * half + side, pl.ds(source, 1), :], (8, 128)
                )
                for side in range(2)
            ],
            axis=1,
        )
        scale, terms, centre_scale = (
            (0.5 / XA, SMALL_TURN, cell_scale),
            (0.5 / ROWS, QUARTER_TURN, row_scale),
        )[axis]
        a_cos, a_sin = unit_turns(reduced(where * centre_scale), ANY_TURN)
        b_cos, b_sin = unit_turns(where * scale, terms)
        cc, ss = a_cos * b_cos, a_sin * b_sin
        sc, cs = a_sin * b_cos, a_cos * b_sin
        return (cc + ss, sc - cs), (cc - ss, sc + cs), double_cos((b_cos, b_sin))

    def make_phases(step, part):
        below, above, twice = beside(step, part, 0)
        pieces = [[None] * 8, [None] * 8]
        for direction in (-1, 1):
            last, before, at = (below, above, 3) if direction < 0 else (above, below, 4)
            while True:
                following = step_on(last, before, twice)
                pair = (following, last) if direction < 0 else (last, following)
                for kind in range(2):
                    pieces[kind][at] = jnp.concatenate(
                        [pair[0][kind], pair[1][kind]], axis=0
                    ).astype(BF16)
                at += direction
                if not 0 <= at < 8:
                    break
                before, last = following, step_on(following, last, twice)
        return pieces[0] + pieces[1]

    def evaluate(step, part, inner):
        below, above, twice = beside(step, part, 1)
        total_real = total_imag = 0.0
        for j in (1, 0, 2, 3):
            if j == 0:
                cosk, sink = step_on(below, above, twice)
            elif j == 3:
                cosk, sink = step_on(above, below, twice)
            else:
                cosk, sink = below if j == 1 else above
            mine = []
            for at in range(8 * j, 8 * j + 128, 32):
                constant = bias[at : at + 8, :]
                mine.append(inner[at : at + 8] + jnp.concatenate([constant, constant], axis=1))
            total_real += mine[0] * cosk - mine[1] * sink
            total_imag += mine[2] * cosk + mine[3] * sink
        return total_real, total_imag

    steps = 2 * SUBS // PARTS

    def fill(made, buffer):
        for number, piece in enumerate(made):
            buffer[16 * number : 16 * number + 16, :] = piece

    def turn(step, ready, following):
        later = jnp.minimum(step + 1, steps - 1)
        inners = [
            jnp.dot(weights[...], ready[part][...], preferred_element_type=F32)
            for part in range(PARTS)
        ]
        made = [make_phases(later, part) for part in range(PARTS)]
        sums = [evaluate(step, part, inners[part]) for part in range(PARTS)]
        for part in range(PARTS):
            fill(made[part], following[part])
            source, half = place(step, part)
            for axis in range(2):
                partial[axis, half, source] = sums[part][axis]

    def both(pair, carry):
        turn(2 * pair, first, second)
        turn(2 * pair + 1, second, first)
        return carry

    first, second = buffers[:PARTS], buffers[PARTS:]
    for part in range(PARTS):
        fill(make_phases(0, part), first[part])
    lax.fori_loop(0, steps // 2, both, 0)
    for half in range(2):
        where = jnp.concatenate([coords[0, 2 * half], coords[0, 2 * half + 1]], axis=1)
        back_cos, back_sin = unit_turns(where * (0.5 / ROWS), QUARTER_TURN)
        real_sum, imag_sum = (
            sum(partial[axis, half, :, i, :] for i in range(8)) * (1.0 / 128.0) for axis in range(2)
        )
        for axis, value in enumerate(
            (real_sum * back_cos + imag_sum * back_sin, imag_sum * back_cos - real_sum * back_sin)
        ):
            at = 4 * axis + 2 * half
            values[:, at, :] = value[:, :128]
            values[:, at + 1, :] = value[:, 128:]
    out_ref[...] = values[...].astype(BF16)


def unpack_kernel(returned_ref, owners_ref, position_ref, out_ref, values):
    values[...] = returned_ref[...].astype(F32)
    table = jnp.concatenate(
        [
            jnp.concatenate([values[:, at, :], values[:, at + 1, :]], axis=1)
            for at in range(0, 8, 2)
        ],
        axis=0,
    ).astype(BF16)
    width = 512
    owner_of = iota((2 * SUBS, width), 0) % SUBS
    start_of = iota((2 * SUBS, width), 0) // SUBS * 256
    slot_of = iota((256, width), 0)
    for block in range(DEV_ROWS // width):
        lanes = pl.ds(block * width, width)
        position = position_ref[:, lanes]
        late = position // 256 * 256
        match = (owners_ref[:, lanes] == owner_of) & (late == start_of)
        slots = (slot_of == position - late).astype(F32).astype(BF16)
        picked = jnp.dot(table, slots, preferred_element_type=F32)
        for axis in range(2):
            out_ref[axis : axis + 1, lanes] = jnp.sum(
                jnp.where(match, picked[64 * axis : 64 * axis + 64], 0.0), axis=0, keepdims=True
            )


def vmem():
    return pl.BlockSpec(memory_space=pltpu.VMEM)


def call(kernel, out_shape, in_specs, scratch, flops, *operands):
    return pl.pallas_call(
        kernel,
        out_shape=out_shape,
        in_specs=in_specs,
        out_specs=jax.tree.map(lambda _: vmem(), out_shape),
        scratch_shapes=scratch,
        compiler_params=pltpu.CompilerParams(vmem_limit_bytes=40 * 1024 * 1024),
        cost_estimate=pl.CostEstimate(flops=flops, bytes_accessed=1 << 20, transcendentals=0),
    )(*operands)


def per_device(facets, taper_weight, offsets, point_coords, owners):
    facet_index = lax.axis_index("facet")
    image = call(
        spread_kernel,
        jax.ShapeDtypeStruct((8, 64, 128), F32),
        [vmem()],
        [pltpu.VMEM((64, 128), F32)],
        0,
        facets,
    )
    image = lax.all_to_all(image, "facet", split_axis=0, concat_axis=0, tiled=True)
    owner_row = owners.reshape(1, DEV_ROWS)
    packed, position = call(
        pack_kernel,
        (
            jax.ShapeDtypeStruct((SUBS, 16, 128), F32),
            jax.ShapeDtypeStruct((1, DEV_ROWS), jnp.int32),
        ),
        [vmem()] * 2,
        [],
        1 << 32,
        point_coords,
        owner_row,
    )
    starts = lax.dynamic_slice(offsets, (facet_index * SUBS,), (SUBS,))
    outer_h, outer_l, twiddle, inner_h, inner_l = transform_tables()
    payload = call(
        window_kernel,
        jax.ShapeDtypeStruct((SUBS, 24, 128), BF16),
        [pl.BlockSpec(memory_space=pltpu.SMEM)] + [vmem()] * 8,
        [
            pltpu.VMEM((2, 128, 256), F32),
            pltpu.VMEM((256, 4, 256), F32),
            pltpu.VMEM((SUBS, 24, 128), F32),
        ],
        1 << 32,
        starts,
        image,
        taper_weight.reshape(16, 128),
        packed,
        outer_h,
        outer_l,
        twiddle,
        inner_h,
        inner_l,
    )
    arrived = lax.all_to_all(payload, "sub", split_axis=0, concat_axis=0, tiled=True)
    values = call(
        degrid_kernel,
        jax.ShapeDtypeStruct((SUBS, 8, 128), BF16),
        [vmem()] * 4,
        [
            pltpu.VMEM((SUBS, 24, 128), F32),
            pltpu.VMEM((2, 4, SUBS, 128), F32),
            pltpu.VMEM((128, 256), BF16),
            pltpu.VMEM((128, 128), F32),
            pltpu.VMEM((2, 2, SUBS, 8, 256), F32),
            pltpu.VMEM((SUBS, 8, 128), F32),
        ]
        + [pltpu.VMEM((256, 256), BF16)] * (2 * PARTS),
        1 << 32,
        arrived,
        *fold_tables(),
    )
    returned = lax.all_to_all(values, "sub", split_axis=0, concat_axis=0, tiled=True)
    return call(
        unpack_kernel,
        jax.ShapeDtypeStruct((2, DEV_ROWS), F32),
        [vmem()] * 3,
        [pltpu.VMEM((SUBS, 8, 128), F32)],
        1 << 32,
        returned,
        owner_row,
        position,
    )


def solution(mesh):
    placed = (
        P("facet", None, "sub", None),
        P(),
        P(),
        P(None, ("facet", "sub")),
        P(("facet", "sub"), None),
    )
    return jax.shard_map(
        per_device, mesh=mesh, in_specs=placed, out_specs=P(None, ("facet", "sub")), check_vma=False
    )
```

```python
import math

import jax
import jax.numpy as jnp
import ml_dtypes
import numpy as np
from jax import lax
from jax.experimental import pallas as pl
from jax.experimental.pallas import tpu as pltpu
from jax.sharding import PartitionSpec as P

N_IMG = 65536
XA = 256
ROWS = 64
SUBS = 32
CAP = 512
DEV_ROWS = 4096
PARTS = 4
F32 = jnp.float32
BF16 = jnp.bfloat16


def split_host(table):
    table = np.asarray(table, np.float32)
    high = table.astype(ml_dtypes.bfloat16)
    low = (table - high.astype(np.float32)).astype(ml_dtypes.bfloat16)
    return high, low


def transform_tables():
    turn = 2.0 * np.pi / 256.0
    a, q = np.arange(64), np.arange(256)
    first = np.outer(a, q) % 256 * turn
    real, imag = np.cos(first), -np.sin(first)
    outer = np.block([[real, imag], [-imag, real]])
    angle = np.outer(q, q) * (2.0 * np.pi / N_IMG)
    twiddle = np.stack([np.cos(angle), -np.sin(angle)]) / 128.0
    second = np.outer(q, q) % 256 * turn
    real, imag = np.cos(second), -np.sin(second)
    inner = np.stack([real, imag], axis=1).astype(np.float32)
    return inner, split_host(outer) + (twiddle.astype(np.float32),)


def fold_tables():
    order = [16 * h + 1 + j for j in range(16) for h in range(8)]
    cells = np.zeros((XA, 3 * 128), np.float32)
    for place, m in enumerate(order):
        if m < 128:
            cells[128 + m, place] += 1.0
            cells[128 + m, 128 + place] += 1.0
        cells[128 - m, place] += 1.0
        cells[128 - m, 128 + place] -= 1.0
    cells[128, 256:] = 1.0
    order = [4 * g + j for j in range(4) for g in range(8)]
    even, odd = np.zeros((2, 32, ROWS), np.float32)
    for place, k in enumerate(order):
        for row, sign in ((32 + k, 1.0), (31 - k, -1.0)):
            at = row % 2 * SUBS + row // 2
            even[place, at], odd[place, at] = 1.0, sign
    none = np.zeros_like(even)
    with_cos = np.block([[even, none], [none, odd], [none, even], [odd, none]])
    with_sin = np.block([[none, -even], [odd, none], [even, none], [none, -odd]])
    return [table.astype(ml_dtypes.bfloat16) for table in (cells, with_cos, with_sin)]


def turn_polynomials(reach, cos_terms, sin_terms):
    nodes = (np.cos(np.pi * (np.arange(400) + 0.5) / 400) + 1.0) / 2.0 * reach**2
    r = np.sqrt(nodes)
    fit = np.polynomial.chebyshev.Chebyshev.fit
    cosine = fit(nodes, np.cos(2 * np.pi * r), cos_terms - 1, domain=[0, reach**2])
    sine = fit(nodes, np.sin(2 * np.pi * r) / r, sin_terms - 1, domain=[0, reach**2])
    plain = np.polynomial.Polynomial
    return (
        [float(c) for c in cosine.convert(kind=plain).coef],
        [float(c) for c in sine.convert(kind=plain).coef],
    )


ANY_TURN = turn_polynomials(0.5, 7, 6)
QUARTER_TURN = turn_polynomials(0.25, 5, 5)
SMALL_TURN = turn_polynomials(0.0625, 4, 3)


def reduced(turns):
    return turns - jnp.round(turns)


def unit_turns(r, terms):
    square = r * r
    cosine, sine = (jnp.full_like(square, part[-1]) for part in terms)
    for term in terms[0][-2::-1]:
        cosine = cosine * square + term
    for term in terms[1][-2::-1]:
        sine = sine * square + term
    return cosine, sine * r


def double_cos(half_step):
    return 2.0 - 4.0 * (half_step[1] * half_step[1])


def step_on(last, before, twice):
    return tuple(twice * x - y for x, y in zip(last, before))


def split_in_kernel(values):
    high = values.astype(BF16)
    return high, (values - high.astype(F32)).astype(BF16)


def iota(shape, axis):
    return lax.broadcasted_iota(jnp.int32, shape, axis)


def pack_kernel(
    starts_ref, coords_ref, owners_ref, inner_ref, packed_ref, position_ref, high_ref, low_ref, chosen
):
    for s in range(SUBS):
        run = starts_ref[s] // 256
        chosen[4 * s : 4 * s + 2, :] = inner_ref[run]
        chosen[4 * s + 2 : 4 * s + 4, :] = inner_ref[(run + 1) % 256]
    high_ref[...], low_ref[...] = split_in_kernel(chosen[...])
    width = 256
    blocks = DEV_ROWS // width
    owner_of = iota((SUBS, width), 0)
    slot_of = iota((CAP, width), 0)
    upper = (iota((width, width), 0) <= iota((width, width), 1)).astype(F32).astype(BF16)
    hots = []
    for block in range(blocks):
        match = owners_ref[:, pl.ds(block * width, width)] == owner_of
        hots.append(match.astype(F32))
    running = jnp.dot(
        jnp.concatenate(hots, axis=0).astype(BF16), upper, preferred_element_type=F32
    )
    carry = jnp.zeros((SUBS, 1), F32)
    positions = []
    for block in range(blocks):
        mine = running[SUBS * block : SUBS * block + SUBS]
        rank = jnp.sum(hots[block] * (mine + carry), axis=0, keepdims=True) - 1.0
        carry = carry + mine[:, width - 1 : width]
        positions.append(rank.astype(jnp.int32))
        position_ref[:, pl.ds(block * width, width)] = positions[-1]
    total = jnp.zeros((4 * SUBS, CAP), F32)
    for block in range(blocks):
        lanes = pl.ds(block * width, width)
        slots = (slot_of == positions[block]).astype(F32).astype(BF16)
        rows = []
        for axis in range(2):
            for piece in split_in_kernel(coords_ref[axis : axis + 1, lanes]):
                rows.append((hots[block] * piece.astype(F32)).astype(BF16))
        total = total + lax.dot_general(
            jnp.concatenate(rows, axis=0),
            slots,
            (((1,), (1,)), ((), ())),
            preferred_element_type=F32,
        )
    for piece in range(4):
        for quarter in range(4):
            packed_ref[:, 4 * piece + quarter, :] = total[
                SUBS * piece : SUBS * piece + SUBS, 128 * quarter : 128 * quarter + 128
            ]


def split_dot(left_pair, right_pair):
    left_high, left_low = left_pair
    right_high, right_low = right_pair
    out = jnp.dot(left_high, right_high, preferred_element_type=F32)
    out = out + jnp.dot(left_low, right_high, preferred_element_type=F32)
    return out + jnp.dot(left_high, right_low, preferred_element_type=F32)


def spread_kernel(facets_ref, out_ref, rows):
    for part in range(2):
        for r in range(2):
            for block in range(16):
                at = 32 * part + 16 * r + block
                rows[at : at + 1, :] = facets_ref[
                    0, part, r : r + 1, 128 * block : 128 * block + 128
                ]
    for f in range(8):
        out_ref[f] = rows[...]


def window_kernel(
    starts_ref,
    image_ref,
    taper_ref,
    packed_ref,
    chosen_h,
    chosen_l,
    outer_h,
    outer_l,
    twiddle_ref,
    out_ref,
    columns,
    payload,
):
    payload[:, 8:24, :] = packed_ref[...]
    reals, imags = [], []
    for r in range(2):
        for part in range(2):
            for f in range(8):
                for side in range(2):
                    line = image_ref[f, pl.ds(32 * part + 16 * r + side, 8, stride=2), :]
                    at = 64 * part + 8 * f
                    columns[r, at : at + 8, 128 * side : 128 * side + 128] = (
                        line * taper_ref[pl.ds(side, 8, stride=2), :]
                    )
        mixed = split_dot(split_in_kernel(columns[r].T), (outer_h[...], outer_l[...]))
        real, imag = mixed[:, :256], mixed[:, 256:]
        turn_real, turn_imag = twiddle_ref[0], twiddle_ref[1]
        reals.append(real * turn_real - imag * turn_imag)
        imags.append(real * turn_imag + imag * turn_real)
    both = jnp.concatenate(reals + imags, axis=1)
    runs = split_dot((chosen_h[...], chosen_l[...]), split_in_kernel(both))
    lane = iota((2, 1024), 1) % 256
    for s in range(SUBS):
        low = starts_ref[s] % 256
        mine = runs[4 * s : 4 * s + 4]
        mine = jnp.where(lane >= low, mine[0:2], mine[2:4])
        real = mine[0:1, :512] - mine[1:2, 512:]
        imag = mine[1:2, :512] + mine[0:1, 512:]
        window = jnp.concatenate([real[:, :256], real[:, 256:], imag[:, :256], imag[:, 256:]], axis=0)
        window = pltpu.roll(window, (256 - low) % 256, 1)
        payload[s, 0:4, :] = window[:, :128]
        payload[s, 4:8, :] = window[:, 128:]
    out_ref[...] = payload[...].astype(BF16)


def degrid_kernel(
    arrived_ref, cells_ref, with_cos_ref, with_sin_ref, out_ref, arrived, coords, weights, bias, partial, values, *buffers
):
    arrived[...] = arrived_ref[...].astype(F32)
    grid = jnp.concatenate(
        [
            jnp.concatenate([arrived[:, 4 * side + plane, :] for plane in range(4)], axis=0)
            for side in range(2)
        ],
        axis=1,
    )
    for axis in range(2):
        for quarter in range(4):
            at = 8 + 8 * axis + quarter
            coords[axis, quarter] = arrived[:, at, :] + arrived[:, at + 4, :]
    by_cell = jnp.dot(grid.astype(BF16), cells_ref[...], preferred_element_type=F32)
    high, low = split_in_kernel(by_cell)

    def fold(matrix, columns):
        return jnp.dot(matrix, high[:, columns], preferred_element_type=F32) + jnp.dot(
            matrix, low[:, columns], preferred_element_type=F32
        )

    weights[:, 0:128] = fold(with_cos_ref[...], slice(0, 128)).astype(BF16)
    weights[:, 128:256] = fold(with_sin_ref[...], slice(128, 256)).astype(BF16)
    bias[...] = fold(with_cos_ref[...], slice(256, 384))

    step_row = iota((8, 256), 0).astype(F32)
    cell_scale = (16.0 * step_row + 8.5) * (1.0 / XA)
    row_scale = (4.0 * step_row + 2.0) * (1.0 / ROWS)
    def place(step, part):
        return (step * PARTS + part) // 2, part % 2

    def beside(step, part, axis):
        source, half = place(step, part)
        where = jnp.concatenate(
            [
                jnp.broadcast_to(
                    coords[1 - axis, 2 * half + side, pl.ds(source, 1), :], (8, 128)
                )
                for side in range(2)
            ],
            axis=1,
        )
        scale, terms, centre_scale = (
            (0.5 / XA, SMALL_TURN, cell_scale),
            (0.5 / ROWS, QUARTER_TURN, row_scale),
        )[axis]
        a_cos, a_sin = unit_turns(reduced(where * centre_scale), ANY_TURN)
        b_cos, b_sin = unit_turns(where * scale, terms)
        cc, ss = a_cos * b_cos, a_sin * b_sin
        sc, cs = a_sin * b_cos, a_cos * b_sin
        return (cc + ss, sc - cs), (cc - ss, sc + cs), double_cos((b_cos, b_sin))

    def make_phases(step, part):
        below, above, twice = beside(step, part, 0)
        pieces = [[None] * 8, [None] * 8]
        for direction in (-1, 1):
            last, before, at = (below, above, 3) if direction < 0 else (above, below, 4)
            while True:
                following = step_on(last, before, twice)
                pair = (following, last) if direction < 0 else (last, following)
                for kind in range(2):
                    pieces[kind][at] = jnp.concatenate(
                        [pair[0][kind], pair[1][kind]], axis=0
                    ).astype(BF16)
                at += direction
                if not 0 <= at < 8:
                    break
                before, last = following, step_on(following, last, twice)
        return pieces[0] + pieces[1]

    def evaluate(step, part, inner):
        below, above, twice = beside(step, part, 1)
        total_real = total_imag = 0.0
        for j in (1, 0, 2, 3):
            if j == 0:
                cosk, sink = step_on(below, above, twice)
            elif j == 3:
                cosk, sink = step_on(above, below, twice)
            else:
                cosk, sink = below if j == 1 else above
            mine = []
            for at in range(8 * j, 8 * j + 128, 32):
                constant = bias[at : at + 8, :]
                mine.append(inner[at : at + 8] + jnp.concatenate([constant, constant], axis=1))
            total_real += mine[0] * cosk - mine[1] * sink
            total_imag += mine[2] * cosk + mine[3] * sink
        return total_real, total_imag

    steps = 2 * SUBS // PARTS

    def fill(made, buffer):
        for number, piece in enumerate(made):
            buffer[16 * number : 16 * number + 16, :] = piece

    def turn(step, ready, following):
        later = jnp.minimum(step + 1, steps - 1)
        inners = [
            jnp.dot(weights[...], ready[part][...], preferred_element_type=F32)
            for part in range(PARTS)
        ]
        made = [make_phases(later, part) for part in range(PARTS)]
        sums = [evaluate(step, part, inners[part]) for part in range(PARTS)]
        for part in range(PARTS):
            fill(made[part], following[part])
            source, half = place(step, part)
            for axis in range(2):
                partial[axis, half, source] = sums[part][axis]

    def both(pair, carry):
        turn(2 * pair, first, second)
        turn(2 * pair + 1, second, first)
        return carry

    first, second = buffers[:PARTS], buffers[PARTS:]
    for part in range(PARTS):
        fill(make_phases(0, part), first[part])
    lax.fori_loop(0, steps // 2, both, 0)
    for half in range(2):
        where = jnp.concatenate([coords[0, 2 * half], coords[0, 2 * half + 1]], axis=1)
        back_cos, back_sin = unit_turns(where * (0.5 / ROWS), QUARTER_TURN)
        real_sum, imag_sum = (
            sum(partial[axis, half, :, i, :] for i in range(8)) * (1.0 / 128.0) for axis in range(2)
        )
        for axis, value in enumerate(
            (real_sum * back_cos + imag_sum * back_sin, imag_sum * back_cos - real_sum * back_sin)
        ):
            at = 4 * axis + 2 * half
            values[:, at, :] = value[:, :128]
            values[:, at + 1, :] = value[:, 128:]
    out_ref[...] = values[...].astype(BF16)


def unpack_kernel(returned_ref, owners_ref, position_ref, out_ref, values):
    values[...] = returned_ref[...].astype(F32)
    table = jnp.concatenate(
        [
            jnp.concatenate([values[:, at, :], values[:, at + 1, :]], axis=1)
            for at in range(0, 8, 2)
        ],
        axis=0,
    ).astype(BF16)
    width = 512
    owner_of = iota((2 * SUBS, width), 0) % SUBS
    start_of = iota((2 * SUBS, width), 0) // SUBS * 256
    slot_of = iota((256, width), 0)
    for block in range(DEV_ROWS // width):
        lanes = pl.ds(block * width, width)
        position = position_ref[:, lanes]
        late = position // 256 * 256
        match = (owners_ref[:, lanes] == owner_of) & (late == start_of)
        slots = (slot_of == position - late).astype(F32).astype(BF16)
        picked = jnp.dot(table, slots, preferred_element_type=F32)
        for axis in range(2):
            out_ref[axis : axis + 1, lanes] = jnp.sum(
                jnp.where(match, picked[64 * axis : 64 * axis + 64], 0.0), axis=0, keepdims=True
            )


def vmem():
    return pl.BlockSpec(memory_space=pltpu.VMEM)


def smem():
    return pl.BlockSpec(memory_space=pltpu.SMEM)


def call(kernel, out_shape, in_specs, scratch, flops, *operands):
    return pl.pallas_call(
        kernel,
        out_shape=out_shape,
        in_specs=in_specs,
        out_specs=jax.tree.map(lambda _: vmem(), out_shape),
        scratch_shapes=scratch,
        compiler_params=pltpu.CompilerParams(vmem_limit_bytes=40 * 1024 * 1024),
        cost_estimate=pl.CostEstimate(flops=flops, bytes_accessed=1 << 20, transcendentals=0),
    )(*operands)


def per_device(facets, taper_weight, offsets, point_coords, owners):
    facet_index = lax.axis_index("facet")
    image = call(
        spread_kernel,
        jax.ShapeDtypeStruct((8, 64, 128), F32),
        [vmem()],
        [pltpu.VMEM((64, 128), F32)],
        0,
        facets,
    )
    image = lax.all_to_all(image, "facet", split_axis=0, concat_axis=0, tiled=True)
    owner_row = owners.reshape(1, DEV_ROWS)
    starts = lax.dynamic_slice(offsets, (facet_index * SUBS,), (SUBS,))
    inner, tables = transform_tables()
    packed, position, chosen_h, chosen_l = call(
        pack_kernel,
        (
            jax.ShapeDtypeStruct((SUBS, 16, 128), F32),
            jax.ShapeDtypeStruct((1, DEV_ROWS), jnp.int32),
            jax.ShapeDtypeStruct((128, 256), BF16),
            jax.ShapeDtypeStruct((128, 256), BF16),
        ),
        [smem()] + [vmem()] * 3,
        [pltpu.VMEM((128, 256), F32)],
        1 << 32,
        starts,
        point_coords,
        owner_row,
        inner,
    )
    payload = call(
        window_kernel,
        jax.ShapeDtypeStruct((SUBS, 24, 128), BF16),
        [smem()] + [vmem()] * 8,
        [pltpu.VMEM((2, 128, 256), F32), pltpu.VMEM((SUBS, 24, 128), F32)],
        1 << 32,
        starts,
        image,
        taper_weight.reshape(16, 128),
        packed,
        chosen_h,
        chosen_l,
        *tables,
    )
    arrived = lax.all_to_all(payload, "sub", split_axis=0, concat_axis=0, tiled=True)
    values = call(
        degrid_kernel,
        jax.ShapeDtypeStruct((SUBS, 8, 128), BF16),
        [vmem()] * 4,
        [
            pltpu.VMEM((SUBS, 24, 128), F32),
            pltpu.VMEM((2, 4, SUBS, 128), F32),
            pltpu.VMEM((128, 256), BF16),
            pltpu.VMEM((128, 128), F32),
            pltpu.VMEM((2, 2, SUBS, 8, 256), F32),
            pltpu.VMEM((SUBS, 8, 128), F32),
        ]
        + [pltpu.VMEM((256, 256), BF16)] * (2 * PARTS),
        1 << 32,
        arrived,
        *fold_tables(),
    )
    returned = lax.all_to_all(values, "sub", split_axis=0, concat_axis=0, tiled=True)
    return call(
        unpack_kernel,
        jax.ShapeDtypeStruct((2, DEV_ROWS), F32),
        [vmem()] * 3,
        [pltpu.VMEM((SUBS, 8, 128), F32)],
        1 << 32,
        returned,
        owner_row,
        position,
    )


def solution(mesh):
    placed = (
        P("facet", None, "sub", None),
        P(),
        P(),
        P(None, ("facet", "sub")),
        P(("facet", "sub"), None),
    )
    return jax.shard_map(
        per_device, mesh=mesh, in_specs=placed, out_specs=P(None, ("facet", "sub")), check_vma=False
    )
```

```python
import math

import jax
import jax.numpy as jnp
import ml_dtypes
import numpy as np
from jax import lax
from jax.experimental import pallas as pl
from jax.experimental.pallas import tpu as pltpu
from jax.sharding import PartitionSpec as P

N_IMG = 65536
XA = 256
ROWS = 64
SUBS = 32
CAP = 512
DEV_ROWS = 4096
PARTS = 4
F32 = jnp.float32
BF16 = jnp.bfloat16


def split_host(table):
    table = np.asarray(table, np.float32)
    high = table.astype(ml_dtypes.bfloat16)
    low = (table - high.astype(np.float32)).astype(ml_dtypes.bfloat16)
    return high, low


def transform_tables():
    turn = 2.0 * np.pi / 256.0
    a, q = np.arange(64), np.arange(256)
    first = np.outer(a, q) % 256 * turn
    real, imag = np.cos(first), -np.sin(first)
    outer = np.block([[real, imag], [-imag, real]])
    angle = np.outer(q, q) * (2.0 * np.pi / N_IMG)
    twiddle = np.stack([np.cos(angle), -np.sin(angle)]) / 128.0
    second = np.outer(q, q) % 256 * turn
    real, imag = np.cos(second), -np.sin(second)
    inner = np.stack([real, imag], axis=1).astype(np.float32)
    return inner, split_host(outer) + (twiddle.astype(np.float32),)


def fold_tables():
    order = [16 * h + 1 + j for j in range(16) for h in range(8)]
    cells = np.zeros((XA, 3 * 128), np.float32)
    for place, m in enumerate(order):
        if m < 128:
            cells[128 + m, place] += 1.0
            cells[128 + m, 128 + place] += 1.0
        cells[128 - m, place] += 1.0
        cells[128 - m, 128 + place] -= 1.0
    cells[128, 256:] = 1.0
    order = [4 * g + j for j in range(4) for g in range(8)]
    even, odd = np.zeros((2, 32, ROWS), np.float32)
    for place, k in enumerate(order):
        for row, sign in ((32 + k, 1.0), (31 - k, -1.0)):
            at = row % 2 * SUBS + row // 2
            even[place, at], odd[place, at] = 1.0, sign
    none = np.zeros_like(even)
    with_cos = np.block([[even, none], [none, odd], [none, even], [odd, none]])
    with_sin = np.block([[none, -even], [odd, none], [even, none], [none, -odd]])
    return [table.astype(ml_dtypes.bfloat16) for table in (cells, with_cos, with_sin)]


def turn_polynomials(reach, cos_terms, sin_terms):
    nodes = (np.cos(np.pi * (np.arange(400) + 0.5) / 400) + 1.0) / 2.0 * reach**2
    r = np.sqrt(nodes)
    fit = np.polynomial.chebyshev.Chebyshev.fit
    cosine = fit(nodes, np.cos(2 * np.pi * r), cos_terms - 1, domain=[0, reach**2])
    sine = fit(nodes, np.sin(2 * np.pi * r) / r, sin_terms - 1, domain=[0, reach**2])
    plain = np.polynomial.Polynomial
    return (
        [float(c) for c in cosine.convert(kind=plain).coef],
        [float(c) for c in sine.convert(kind=plain).coef],
    )


ANY_TURN = turn_polynomials(0.5, 7, 6)
QUARTER_TURN = turn_polynomials(0.25, 5, 5)
SMALL_TURN = turn_polynomials(0.0625, 4, 3)


def reduced(turns):
    return turns - jnp.round(turns)


def unit_turns(r, terms):
    square = r * r
    cosine, sine = (jnp.full_like(square, part[-1]) for part in terms)
    for term in terms[0][-2::-1]:
        cosine = cosine * square + term
    for term in terms[1][-2::-1]:
        sine = sine * square + term
    return cosine, sine * r


def double_cos(half_step):
    return 2.0 - 4.0 * (half_step[1] * half_step[1])


def step_on(last, before, twice):
    return tuple(twice * x - y for x, y in zip(last, before))


def split_in_kernel(values):
    high = values.astype(BF16)
    return high, (values - high.astype(F32)).astype(BF16)


def iota(shape, axis):
    return lax.broadcasted_iota(jnp.int32, shape, axis)


def pack_kernel(
    starts_ref, coords_ref, owners_ref, inner_ref, packed_ref, position_ref, slots_ref, high_ref, low_ref, chosen
):
    for s in range(SUBS):
        run = starts_ref[s] // 256
        chosen[4 * s : 4 * s + 2, :] = inner_ref[run]
        chosen[4 * s + 2 : 4 * s + 4, :] = inner_ref[(run + 1) % 256]
    high_ref[...], low_ref[...] = split_in_kernel(chosen[...])
    width = 256
    blocks = DEV_ROWS // width
    owner_of = iota((SUBS, width), 0)
    slot_of = iota((CAP, width), 0)
    upper = (iota((width, width), 0) <= iota((width, width), 1)).astype(F32).astype(BF16)
    hots = []
    for block in range(blocks):
        match = owners_ref[:, pl.ds(block * width, width)] == owner_of
        hots.append(match.astype(F32))
    running = jnp.dot(
        jnp.concatenate(hots, axis=0).astype(BF16), upper, preferred_element_type=F32
    )
    carry = jnp.zeros((SUBS, 1), F32)
    positions = []
    for block in range(blocks):
        mine = running[SUBS * block : SUBS * block + SUBS]
        rank = jnp.sum(hots[block] * (mine + carry), axis=0, keepdims=True) - 1.0
        carry = carry + mine[:, width - 1 : width]
        positions.append(rank.astype(jnp.int32))
        lanes = pl.ds(block * width, width)
        position_ref[:, lanes] = positions[-1]
        own_slots = (iota((256, width), 0) == positions[-1] % 256).astype(F32)
        slots_ref[:, lanes] = own_slots.astype(BF16)
    total = jnp.zeros((4 * SUBS, CAP), F32)
    for block in range(blocks):
        lanes = pl.ds(block * width, width)
        slots = (slot_of == positions[block]).astype(F32).astype(BF16)
        rows = []
        for axis in range(2):
            for piece in split_in_kernel(coords_ref[axis : axis + 1, lanes]):
                rows.append((hots[block] * piece.astype(F32)).astype(BF16))
        total = total + lax.dot_general(
            jnp.concatenate(rows, axis=0),
            slots,
            (((1,), (1,)), ((), ())),
            preferred_element_type=F32,
        )
    for piece in range(4):
        for quarter in range(4):
            packed_ref[:, 4 * piece + quarter, :] = total[
                SUBS * piece : SUBS * piece + SUBS, 128 * quarter : 128 * quarter + 128
            ]


def split_dot(left_pair, right_pair):
    left_high, left_low = left_pair
    right_high, right_low = right_pair
    out = jnp.dot(left_high, right_high, preferred_element_type=F32)
    out = out + jnp.dot(left_low, right_high, preferred_element_type=F32)
    return out + jnp.dot(left_high, right_low, preferred_element_type=F32)


def spread_kernel(facets_ref, out_ref, rows):
    for part in range(2):
        for r in range(2):
            for block in range(16):
                at = 32 * part + 16 * r + block
                rows[at : at + 1, :] = facets_ref[
                    0, part, r : r + 1, 128 * block : 128 * block + 128
                ]
    for f in range(8):
        out_ref[f] = rows[...]


def window_kernel(
    starts_ref,
    image_ref,
    taper_ref,
    packed_ref,
    chosen_h,
    chosen_l,
    outer_h,
    outer_l,
    twiddle_ref,
    out_ref,
    columns,
    payload,
):
    payload[:, 8:24, :] = packed_ref[...]
    reals, imags = [], []
    for r in range(2):
        for part in range(2):
            for f in range(8):
                for side in range(2):
                    line = image_ref[f, pl.ds(32 * part + 16 * r + side, 8, stride=2), :]
                    at = 64 * part + 8 * f
                    columns[r, at : at + 8, 128 * side : 128 * side + 128] = (
                        line * taper_ref[pl.ds(side, 8, stride=2), :]
                    )
        mixed = split_dot(split_in_kernel(columns[r].T), (outer_h[...], outer_l[...]))
        real, imag = mixed[:, :256], mixed[:, 256:]
        turn_real, turn_imag = twiddle_ref[0], twiddle_ref[1]
        reals.append(real * turn_real - imag * turn_imag)
        imags.append(real * turn_imag + imag * turn_real)
    both = jnp.concatenate(reals + imags, axis=1)
    runs = split_dot((chosen_h[...], chosen_l[...]), split_in_kernel(both))
    lane = iota((2, 1024), 1) % 256
    for s in range(SUBS):
        low = starts_ref[s] % 256
        mine = runs[4 * s : 4 * s + 4]
        mine = jnp.where(lane >= low, mine[0:2], mine[2:4])
        real = mine[0:1, :512] - mine[1:2, 512:]
        imag = mine[1:2, :512] + mine[0:1, 512:]
        window = jnp.concatenate([real[:, :256], real[:, 256:], imag[:, :256], imag[:, 256:]], axis=0)
        window = pltpu.roll(window, (256 - low) % 256, 1)
        payload[s, 0:4, :] = window[:, :128]
        payload[s, 4:8, :] = window[:, 128:]
    out_ref[...] = payload[...].astype(BF16)


def degrid_kernel(
    arrived_ref, cells_ref, with_cos_ref, with_sin_ref, out_ref, arrived, coords, weights, bias, partial, values, *buffers
):
    arrived[...] = arrived_ref[...].astype(F32)
    grid = jnp.concatenate(
        [
            jnp.concatenate([arrived[:, 4 * side + plane, :] for plane in range(4)], axis=0)
            for side in range(2)
        ],
        axis=1,
    )
    for axis in range(2):
        for quarter in range(4):
            at = 8 + 8 * axis + quarter
            coords[axis, quarter] = arrived[:, at, :] + arrived[:, at + 4, :]
    by_cell = jnp.dot(grid.astype(BF16), cells_ref[...], preferred_element_type=F32)
    high, low = split_in_kernel(by_cell)

    def fold(matrix, columns):
        return jnp.dot(matrix, high[:, columns], preferred_element_type=F32) + jnp.dot(
            matrix, low[:, columns], preferred_element_type=F32
        )

    weights[:, 0:128] = fold(with_cos_ref[...], slice(0, 128)).astype(BF16)
    weights[:, 128:256] = fold(with_sin_ref[...], slice(128, 256)).astype(BF16)
    bias[...] = fold(with_cos_ref[...], slice(256, 384))

    step_row = iota((8, 256), 0).astype(F32)
    cell_scale = (16.0 * step_row + 8.5) * (1.0 / XA)
    row_scale = (4.0 * step_row + 2.0) * (1.0 / ROWS)
    def place(step, part):
        return (step * PARTS + part) // 2, part % 2

    def beside(step, part, axis):
        source, half = place(step, part)
        where = jnp.concatenate(
            [
                jnp.broadcast_to(
                    coords[1 - axis, 2 * half + side, pl.ds(source, 1), :], (8, 128)
                )
                for side in range(2)
            ],
            axis=1,
        )
        scale, terms, centre_scale = (
            (0.5 / XA, SMALL_TURN, cell_scale),
            (0.5 / ROWS, QUARTER_TURN, row_scale),
        )[axis]
        a_cos, a_sin = unit_turns(reduced(where * centre_scale), ANY_TURN)
        b_cos, b_sin = unit_turns(where * scale, terms)
        cc, ss = a_cos * b_cos, a_sin * b_sin
        sc, cs = a_sin * b_cos, a_cos * b_sin
        return (cc + ss, sc - cs), (cc - ss, sc + cs), double_cos((b_cos, b_sin))

    def make_phases(step, part):
        below, above, twice = beside(step, part, 0)
        pieces = [[None] * 8, [None] * 8]
        for direction in (-1, 1):
            last, before, at = (below, above, 3) if direction < 0 else (above, below, 4)
            while True:
                following = step_on(last, before, twice)
                pair = (following, last) if direction < 0 else (last, following)
                for kind in range(2):
                    pieces[kind][at] = jnp.concatenate(
                        [pair[0][kind], pair[1][kind]], axis=0
                    ).astype(BF16)
                at += direction
                if not 0 <= at < 8:
                    break
                before, last = following, step_on(following, last, twice)
        return pieces[0] + pieces[1]

    def evaluate(step, part, inner):
        below, above, twice = beside(step, part, 1)
        total_real = total_imag = 0.0
        for j in (1, 0, 2, 3):
            if j == 0:
                cosk, sink = step_on(below, above, twice)
            elif j == 3:
                cosk, sink = step_on(above, below, twice)
            else:
                cosk, sink = below if j == 1 else above
            mine = []
            for at in range(8 * j, 8 * j + 128, 32):
                constant = bias[at : at + 8, :]
                mine.append(inner[at : at + 8] + jnp.concatenate([constant, constant], axis=1))
            total_real += mine[0] * cosk - mine[1] * sink
            total_imag += mine[2] * cosk + mine[3] * sink
        return total_real, total_imag

    steps = 2 * SUBS // PARTS

    def fill(made, buffer):
        for number, piece in enumerate(made):
            buffer[16 * number : 16 * number + 16, :] = piece

    def turn(step, ready, following):
        later = jnp.minimum(step + 1, steps - 1)
        inners = [
            jnp.dot(weights[...], ready[part][...], preferred_element_type=F32)
            for part in range(PARTS)
        ]
        made = [make_phases(later, part) for part in range(PARTS)]
        sums = [evaluate(step, part, inners[part]) for part in range(PARTS)]
        for part in range(PARTS):
            fill(made[part], following[part])
            source, half = place(step, part)
            for axis in range(2):
                partial[axis, half, source] = sums[part][axis]

    def both(pair, carry):
        turn(2 * pair, first, second)
        turn(2 * pair + 1, second, first)
        return carry

    first, second = buffers[:PARTS], buffers[PARTS:]
    for part in range(PARTS):
        fill(make_phases(0, part), first[part])
    lax.fori_loop(0, steps // 2, both, 0)
    for half in range(2):
        where = jnp.concatenate([coords[0, 2 * half], coords[0, 2 * half + 1]], axis=1)
        back_cos, back_sin = unit_turns(where * (0.5 / ROWS), QUARTER_TURN)
        real_sum, imag_sum = (
            sum(partial[axis, half, :, i, :] for i in range(8)) * (1.0 / 128.0) for axis in range(2)
        )
        for axis, value in enumerate(
            (real_sum * back_cos + imag_sum * back_sin, imag_sum * back_cos - real_sum * back_sin)
        ):
            at = 4 * axis + 2 * half
            values[:, at, :] = value[:, :128]
            values[:, at + 1, :] = value[:, 128:]
    out_ref[...] = values[...].astype(BF16)


def unpack_kernel(returned_ref, owners_ref, position_ref, slots_ref, out_ref, values):
    values[...] = returned_ref[...].astype(F32)
    table = jnp.concatenate(
        [
            jnp.concatenate([values[:, at, :], values[:, at + 1, :]], axis=1)
            for at in range(0, 8, 2)
        ],
        axis=0,
    ).astype(BF16)
    width = 512
    owner_of = iota((2 * SUBS, width), 0) % SUBS
    late_of = iota((2 * SUBS, width), 0) // SUBS
    for block in range(DEV_ROWS // width):
        lanes = pl.ds(block * width, width)
        match = (owners_ref[:, lanes] == owner_of) & (position_ref[:, lanes] // 256 == late_of)
        picked = jnp.dot(table, slots_ref[:, lanes], preferred_element_type=F32)
        for axis in range(2):
            out_ref[axis : axis + 1, lanes] = jnp.sum(
                jnp.where(match, picked[64 * axis : 64 * axis + 64], 0.0), axis=0, keepdims=True
            )


def vmem():
    return pl.BlockSpec(memory_space=pltpu.VMEM)


def smem():
    return pl.BlockSpec(memory_space=pltpu.SMEM)


def call(kernel, out_shape, in_specs, scratch, flops, *operands):
    return pl.pallas_call(
        kernel,
        out_shape=out_shape,
        in_specs=in_specs,
        out_specs=jax.tree.map(lambda _: vmem(), out_shape),
        scratch_shapes=scratch,
        compiler_params=pltpu.CompilerParams(vmem_limit_bytes=40 * 1024 * 1024),
        cost_estimate=pl.CostEstimate(flops=flops, bytes_accessed=1 << 20, transcendentals=0),
    )(*operands)


def per_device(facets, taper_weight, offsets, point_coords, owners):
    facet_index = lax.axis_index("facet")
    image = call(
        spread_kernel,
        jax.ShapeDtypeStruct((8, 64, 128), F32),
        [vmem()],
        [pltpu.VMEM((64, 128), F32)],
        0,
        facets,
    )
    image = lax.all_to_all(image, "facet", split_axis=0, concat_axis=0, tiled=True)
    owner_row = owners.reshape(1, DEV_ROWS)
    starts = lax.dynamic_slice(offsets, (facet_index * SUBS,), (SUBS,))
    inner, tables = transform_tables()
    packed, position, slots, chosen_h, chosen_l = call(
        pack_kernel,
        (
            jax.ShapeDtypeStruct((SUBS, 16, 128), F32),
            jax.ShapeDtypeStruct((1, DEV_ROWS), jnp.int32),
            jax.ShapeDtypeStruct((256, DEV_ROWS), BF16),
            jax.ShapeDtypeStruct((128, 256), BF16),
            jax.ShapeDtypeStruct((128, 256), BF16),
        ),
        [smem()] + [vmem()] * 3,
        [pltpu.VMEM((128, 256), F32)],
        1 << 32,
        starts,
        point_coords,
        owner_row,
        inner,
    )
    payload = call(
        window_kernel,
        jax.ShapeDtypeStruct((SUBS, 24, 128), BF16),
        [smem()] + [vmem()] * 8,
        [pltpu.VMEM((2, 128, 256), F32), pltpu.VMEM((SUBS, 24, 128), F32)],
        1 << 32,
        starts,
        image,
        taper_weight.reshape(16, 128),
        packed,
        chosen_h,
        chosen_l,
        *tables,
    )
    arrived = lax.all_to_all(payload, "sub", split_axis=0, concat_axis=0, tiled=True)
    values = call(
        degrid_kernel,
        jax.ShapeDtypeStruct((SUBS, 8, 128), BF16),
        [vmem()] * 4,
        [
            pltpu.VMEM((SUBS, 24, 128), F32),
            pltpu.VMEM((2, 4, SUBS, 128), F32),
            pltpu.VMEM((128, 256), BF16),
            pltpu.VMEM((128, 128), F32),
            pltpu.VMEM((2, 2, SUBS, 8, 256), F32),
            pltpu.VMEM((SUBS, 8, 128), F32),
        ]
        + [pltpu.VMEM((256, 256), BF16)] * (2 * PARTS),
        1 << 32,
        arrived,
        *fold_tables(),
    )
    returned = lax.all_to_all(values, "sub", split_axis=0, concat_axis=0, tiled=True)
    return call(
        unpack_kernel,
        jax.ShapeDtypeStruct((2, DEV_ROWS), F32),
        [vmem()] * 4,
        [pltpu.VMEM((SUBS, 8, 128), F32)],
        1 << 32,
        returned,
        owner_row,
        position,
        slots,
    )


def solution(mesh):
    placed = (
        P("facet", None, "sub", None),
        P(),
        P(),
        P(None, ("facet", "sub")),
        P(("facet", "sub"), None),
    )
    return jax.shard_map(
        per_device, mesh=mesh, in_specs=placed, out_specs=P(None, ("facet", "sub")), check_vma=False
    )
```

```python
import math

import jax
import jax.numpy as jnp
import ml_dtypes
import numpy as np
from jax import lax
from jax.experimental import pallas as pl
from jax.experimental.pallas import tpu as pltpu
from jax.sharding import PartitionSpec as P

N_IMG = 65536
XA = 256
ROWS = 64
SUBS = 32
CAP = 512
DEV_ROWS = 4096
PARTS = 8
F32 = jnp.float32
BF16 = jnp.bfloat16


def split_host(table):
    table = np.asarray(table, np.float32)
    high = table.astype(ml_dtypes.bfloat16)
    low = (table - high.astype(np.float32)).astype(ml_dtypes.bfloat16)
    return high, low


def transform_tables():
    turn = 2.0 * np.pi / 256.0
    a, q = np.arange(64), np.arange(256)
    first = np.outer(a, q) % 256 * turn
    real, imag = np.cos(first), -np.sin(first)
    outer = np.block([[real, imag], [-imag, real]])
    angle = np.outer(q, q) * (2.0 * np.pi / N_IMG)
    twiddle = np.stack([np.cos(angle), -np.sin(angle)]) / 128.0
    second = np.outer(q, q) % 256 * turn
    real, imag = np.cos(second), -np.sin(second)
    inner = np.stack([real, imag], axis=1).astype(np.float32)
    return inner, split_host(outer) + (twiddle.astype(np.float32),)


def fold_tables():
    order = [16 * h + 1 + j for j in range(16) for h in range(8)]
    cells = np.zeros((XA, 3 * 128), np.float32)
    for place, m in enumerate(order):
        if m < 128:
            cells[128 + m, place] += 1.0
            cells[128 + m, 128 + place] += 1.0
        cells[128 - m, place] += 1.0
        cells[128 - m, 128 + place] -= 1.0
    cells[128, 256:] = 1.0
    order = [4 * g + j for j in range(4) for g in range(8)]
    even, odd = np.zeros((2, 32, ROWS), np.float32)
    for place, k in enumerate(order):
        for row, sign in ((32 + k, 1.0), (31 - k, -1.0)):
            at = row % 2 * SUBS + row // 2
            even[place, at], odd[place, at] = 1.0, sign
    none = np.zeros_like(even)
    with_cos = np.block([[even, none], [none, odd], [none, even], [odd, none]])
    with_sin = np.block([[none, -even], [odd, none], [even, none], [none, -odd]])
    return [table.astype(ml_dtypes.bfloat16) for table in (cells, with_cos, with_sin)]


def turn_polynomials(reach, cos_terms, sin_terms):
    nodes = (np.cos(np.pi * (np.arange(400) + 0.5) / 400) + 1.0) / 2.0 * reach**2
    r = np.sqrt(nodes)
    fit = np.polynomial.chebyshev.Chebyshev.fit
    cosine = fit(nodes, np.cos(2 * np.pi * r), cos_terms - 1, domain=[0, reach**2])
    sine = fit(nodes, np.sin(2 * np.pi * r) / r, sin_terms - 1, domain=[0, reach**2])
    plain = np.polynomial.Polynomial
    return (
        [float(c) for c in cosine.convert(kind=plain).coef],
        [float(c) for c in sine.convert(kind=plain).coef],
    )


ANY_TURN = turn_polynomials(0.5, 7, 6)
QUARTER_TURN = turn_polynomials(0.25, 5, 5)
SMALL_TURN = turn_polynomials(0.0625, 4, 3)


def reduced(turns):
    return turns - jnp.round(turns)


def unit_turns(r, terms):
    square = r * r
    cosine, sine = (jnp.full_like(square, part[-1]) for part in terms)
    for term in terms[0][-2::-1]:
        cosine = cosine * square + term
    for term in terms[1][-2::-1]:
        sine = sine * square + term
    return cosine, sine * r


def double_cos(half_step):
    return 2.0 - 4.0 * (half_step[1] * half_step[1])


def step_on(last, before, twice):
    return tuple(twice * x - y for x, y in zip(last, before))


def split_in_kernel(values):
    high = values.astype(BF16)
    return high, (values - high.astype(F32)).astype(BF16)


def iota(shape, axis):
    return lax.broadcasted_iota(jnp.int32, shape, axis)


def pack_kernel(
    starts_ref, coords_ref, owners_ref, inner_ref, packed_ref, position_ref, slots_ref, high_ref, low_ref, chosen
):
    for s in range(SUBS):
        run = starts_ref[s] // 256
        chosen[4 * s : 4 * s + 2, :] = inner_ref[run]
        chosen[4 * s + 2 : 4 * s + 4, :] = inner_ref[(run + 1) % 256]
    high_ref[...], low_ref[...] = split_in_kernel(chosen[...])
    width = 256
    blocks = DEV_ROWS // width
    owner_of = iota((SUBS, width), 0)
    slot_of = iota((CAP, width), 0)
    upper = (iota((width, width), 0) <= iota((width, width), 1)).astype(F32).astype(BF16)
    hots = []
    for block in range(blocks):
        match = owners_ref[:, pl.ds(block * width, width)] == owner_of
        hots.append(match.astype(F32))
    running = jnp.dot(
        jnp.concatenate(hots, axis=0).astype(BF16), upper, preferred_element_type=F32
    )
    carry = jnp.zeros((SUBS, 1), F32)
    positions = []
    for block in range(blocks):
        mine = running[SUBS * block : SUBS * block + SUBS]
        rank = jnp.sum(hots[block] * (mine + carry), axis=0, keepdims=True) - 1.0
        carry = carry + mine[:, width - 1 : width]
        positions.append(rank.astype(jnp.int32))
        lanes = pl.ds(block * width, width)
        position_ref[:, lanes] = positions[-1]
        own_slots = (iota((256, width), 0) == positions[-1] % 256).astype(F32)
        slots_ref[:, lanes] = own_slots.astype(BF16)
    total = jnp.zeros((4 * SUBS, CAP), F32)
    for block in range(blocks):
        lanes = pl.ds(block * width, width)
        slots = (slot_of == positions[block]).astype(F32).astype(BF16)
        rows = []
        for axis in range(2):
            for piece in split_in_kernel(coords_ref[axis : axis + 1, lanes]):
                rows.append((hots[block] * piece.astype(F32)).astype(BF16))
        total = total + lax.dot_general(
            jnp.concatenate(rows, axis=0),
            slots,
            (((1,), (1,)), ((), ())),
            preferred_element_type=F32,
        )
    for piece in range(4):
        for quarter in range(4):
            packed_ref[:, 4 * piece + quarter, :] = total[
                SUBS * piece : SUBS * piece + SUBS, 128 * quarter : 128 * quarter + 128
            ]


def split_dot(left_pair, right_pair):
    left_high, left_low = left_pair
    right_high, right_low = right_pair
    out = jnp.dot(left_high, right_high, preferred_element_type=F32)
    out = out + jnp.dot(left_low, right_high, preferred_element_type=F32)
    return out + jnp.dot(left_high, right_low, preferred_element_type=F32)


def spread_kernel(facets_ref, out_ref, rows):
    for part in range(2):
        for r in range(2):
            for block in range(16):
                at = 32 * part + 16 * r + block
                rows[at : at + 1, :] = facets_ref[
                    0, part, r : r + 1, 128 * block : 128 * block + 128
                ]
    for f in range(8):
        out_ref[f] = rows[...]


def window_kernel(
    starts_ref,
    image_ref,
    taper_ref,
    packed_ref,
    chosen_h,
    chosen_l,
    outer_h,
    outer_l,
    twiddle_ref,
    out_ref,
    columns,
    payload,
):
    payload[:, 8:24, :] = packed_ref[...]
    reals, imags = [], []
    for r in range(2):
        for part in range(2):
            for f in range(8):
                for side in range(2):
                    line = image_ref[f, pl.ds(32 * part + 16 * r + side, 8, stride=2), :]
                    at = 64 * part + 8 * f
                    columns[r, at : at + 8, 128 * side : 128 * side + 128] = (
                        line * taper_ref[pl.ds(side, 8, stride=2), :]
                    )
        mixed = split_dot(split_in_kernel(columns[r].T), (outer_h[...], outer_l[...]))
        real, imag = mixed[:, :256], mixed[:, 256:]
        turn_real, turn_imag = twiddle_ref[0], twiddle_ref[1]
        reals.append(real * turn_real - imag * turn_imag)
        imags.append(real * turn_imag + imag * turn_real)
    both = jnp.concatenate(reals + imags, axis=1)
    runs = split_dot((chosen_h[...], chosen_l[...]), split_in_kernel(both))
    lane = iota((2, 1024), 1) % 256
    for s in range(SUBS):
        low = starts_ref[s] % 256
        mine = runs[4 * s : 4 * s + 4]
        mine = jnp.where(lane >= low, mine[0:2], mine[2:4])
        real = mine[0:1, :512] - mine[1:2, 512:]
        imag = mine[1:2, :512] + mine[0:1, 512:]
        window = jnp.concatenate([real[:, :256], real[:, 256:], imag[:, :256], imag[:, 256:]], axis=0)
        window = pltpu.roll(window, (256 - low) % 256, 1)
        payload[s, 0:4, :] = window[:, :128]
        payload[s, 4:8, :] = window[:, 128:]
    out_ref[...] = payload[...].astype(BF16)


def degrid_kernel(
    arrived_ref, cells_ref, with_cos_ref, with_sin_ref, out_ref, arrived, coords, weights, bias, partial, values, phases
):
    arrived[...] = arrived_ref[...].astype(F32)
    grid = jnp.concatenate(
        [
            jnp.concatenate([arrived[:, 4 * side + plane, :] for plane in range(4)], axis=0)
            for side in range(2)
        ],
        axis=1,
    )
    for axis in range(2):
        for quarter in range(4):
            at = 8 + 8 * axis + quarter
            coords[axis, quarter] = arrived[:, at, :] + arrived[:, at + 4, :]
    by_cell = jnp.dot(grid.astype(BF16), cells_ref[...], preferred_element_type=F32)
    high, low = split_in_kernel(by_cell)

    def fold(matrix, columns):
        return jnp.dot(matrix, high[:, columns], preferred_element_type=F32) + jnp.dot(
            matrix, low[:, columns], preferred_element_type=F32
        )

    weights[:, 0:128] = fold(with_cos_ref[...], slice(0, 128)).astype(BF16)
    weights[:, 128:256] = fold(with_sin_ref[...], slice(128, 256)).astype(BF16)
    bias[...] = fold(with_cos_ref[...], slice(256, 384))

    step_row = iota((8, 256), 0).astype(F32)
    cell_scale = (16.0 * step_row + 8.5) * (1.0 / XA)
    row_scale = (4.0 * step_row + 2.0) * (1.0 / ROWS)
    def place(step, part):
        return (step * PARTS + part) // 2, part % 2

    def beside(step, part, axis):
        source, half = place(step, part)
        where = jnp.concatenate(
            [
                jnp.broadcast_to(
                    coords[1 - axis, 2 * half + side, pl.ds(source, 1), :], (8, 128)
                )
                for side in range(2)
            ],
            axis=1,
        )
        scale, terms, centre_scale = (
            (0.5 / XA, SMALL_TURN, cell_scale),
            (0.5 / ROWS, QUARTER_TURN, row_scale),
        )[axis]
        a_cos, a_sin = unit_turns(reduced(where * centre_scale), ANY_TURN)
        b_cos, b_sin = unit_turns(where * scale, terms)
        cc, ss = a_cos * b_cos, a_sin * b_sin
        sc, cs = a_sin * b_cos, a_cos * b_sin
        return (cc + ss, sc - cs), (cc - ss, sc + cs), double_cos((b_cos, b_sin))

    def make_phases(step, part):
        below, above, twice = beside(step, part, 0)
        pieces = [[None] * 8, [None] * 8]
        for direction in (-1, 1):
            last, before, at = (below, above, 3) if direction < 0 else (above, below, 4)
            while True:
                following = step_on(last, before, twice)
                pair = (following, last) if direction < 0 else (last, following)
                for kind in range(2):
                    pieces[kind][at] = jnp.concatenate(
                        [pair[0][kind], pair[1][kind]], axis=0
                    ).astype(BF16)
                at += direction
                if not 0 <= at < 8:
                    break
                before, last = following, step_on(following, last, twice)
        return pieces[0] + pieces[1]

    def evaluate(step, part, inner):
        below, above, twice = beside(step, part, 1)
        total_real = total_imag = 0.0
        for j in (1, 0, 2, 3):
            if j == 0:
                cosk, sink = step_on(below, above, twice)
            elif j == 3:
                cosk, sink = step_on(above, below, twice)
            else:
                cosk, sink = below if j == 1 else above
            mine = []
            for at in range(8 * j, 8 * j + 128, 32):
                constant = bias[at : at + 8, :]
                mine.append(inner[at : at + 8] + jnp.concatenate([constant, constant], axis=1))
            total_real += mine[0] * cosk - mine[1] * sink
            total_imag += mine[2] * cosk + mine[3] * sink
        return total_real, total_imag

    steps = 2 * SUBS // PARTS

    def fill(made, buffer):
        for number, piece in enumerate(made):
            buffer[16 * number : 16 * number + 16, :] = piece

    def produce(step, carry):
        for part in range(PARTS):
            fill(make_phases(step, part), phases.at[step * PARTS + part])
        return carry

    def consume(step, carry):
        for part in range(2 * PARTS):
            inner = jnp.dot(
                weights[...], phases[step * 2 * PARTS + part], preferred_element_type=F32
            )
            sums = evaluate(2 * step, part, inner)
            source, half = place(2 * step, part)
            for axis in range(2):
                partial[axis, half, source] = sums[axis]
        return carry

    lax.fori_loop(0, steps, produce, 0)
    lax.fori_loop(0, steps // 2, consume, 0)
    for half in range(2):
        where = jnp.concatenate([coords[0, 2 * half], coords[0, 2 * half + 1]], axis=1)
        back_cos, back_sin = unit_turns(where * (0.5 / ROWS), QUARTER_TURN)
        real_sum, imag_sum = (
            sum(partial[axis, half, :, i, :] for i in range(8)) * (1.0 / 128.0) for axis in range(2)
        )
        for axis, value in enumerate(
            (real_sum * back_cos + imag_sum * back_sin, imag_sum * back_cos - real_sum * back_sin)
        ):
            at = 4 * axis + 2 * half
            values[:, at, :] = value[:, :128]
            values[:, at + 1, :] = value[:, 128:]
    out_ref[...] = values[...].astype(BF16)


def unpack_kernel(returned_ref, owners_ref, position_ref, slots_ref, out_ref, values):
    values[...] = returned_ref[...].astype(F32)
    table = jnp.concatenate(
        [
            jnp.concatenate([values[:, at, :], values[:, at + 1, :]], axis=1)
            for at in range(0, 8, 2)
        ],
        axis=0,
    ).astype(BF16)
    width = 512
    owner_of = iota((2 * SUBS, width), 0) % SUBS
    late_of = iota((2 * SUBS, width), 0) // SUBS
    for block in range(DEV_ROWS // width):
        lanes = pl.ds(block * width, width)
        match = (owners_ref[:, lanes] == owner_of) & (position_ref[:, lanes] // 256 == late_of)
        picked = jnp.dot(table, slots_ref[:, lanes], preferred_element_type=F32)
        for axis in range(2):
            out_ref[axis : axis + 1, lanes] = jnp.sum(
                jnp.where(match, picked[64 * axis : 64 * axis + 64], 0.0), axis=0, keepdims=True
            )


def vmem():
    return pl.BlockSpec(memory_space=pltpu.VMEM)


def smem():
    return pl.BlockSpec(memory_space=pltpu.SMEM)


def call(kernel, out_shape, in_specs, scratch, flops, *operands):
    return pl.pallas_call(
        kernel,
        out_shape=out_shape,
        in_specs=in_specs,
        out_specs=jax.tree.map(lambda _: vmem(), out_shape),
        scratch_shapes=scratch,
        compiler_params=pltpu.CompilerParams(vmem_limit_bytes=40 * 1024 * 1024),
        cost_estimate=pl.CostEstimate(flops=flops, bytes_accessed=1 << 20, transcendentals=0),
    )(*operands)


def per_device(facets, taper_weight, offsets, point_coords, owners):
    facet_index = lax.axis_index("facet")
    image = call(
        spread_kernel,
        jax.ShapeDtypeStruct((8, 64, 128), F32),
        [vmem()],
        [pltpu.VMEM((64, 128), F32)],
        0,
        facets,
    )
    image = lax.all_to_all(image, "facet", split_axis=0, concat_axis=0, tiled=True)
    owner_row = owners.reshape(1, DEV_ROWS)
    starts = lax.dynamic_slice(offsets, (facet_index * SUBS,), (SUBS,))
    inner, tables = transform_tables()
    packed, position, slots, chosen_h, chosen_l = call(
        pack_kernel,
        (
            jax.ShapeDtypeStruct((SUBS, 16, 128), F32),
            jax.ShapeDtypeStruct((1, DEV_ROWS), jnp.int32),
            jax.ShapeDtypeStruct((256, DEV_ROWS), BF16),
            jax.ShapeDtypeStruct((128, 256), BF16),
            jax.ShapeDtypeStruct((128, 256), BF16),
        ),
        [smem()] + [vmem()] * 3,
        [pltpu.VMEM((128, 256), F32)],
        1 << 32,
        starts,
        point_coords,
        owner_row,
        inner,
    )
    payload = call(
        window_kernel,
        jax.ShapeDtypeStruct((SUBS, 24, 128), BF16),
        [smem()] + [vmem()] * 8,
        [pltpu.VMEM((2, 128, 256), F32), pltpu.VMEM((SUBS, 24, 128), F32)],
        1 << 32,
        starts,
        image,
        taper_weight.reshape(16, 128),
        packed,
        chosen_h,
        chosen_l,
        *tables,
    )
    arrived = lax.all_to_all(payload, "sub", split_axis=0, concat_axis=0, tiled=True)
    values = call(
        degrid_kernel,
        jax.ShapeDtypeStruct((SUBS, 8, 128), BF16),
        [vmem()] * 4,
        [
            pltpu.VMEM((SUBS, 24, 128), F32),
            pltpu.VMEM((2, 4, SUBS, 128), F32),
            pltpu.VMEM((128, 256), BF16),
            pltpu.VMEM((128, 128), F32),
            pltpu.VMEM((2, 2, SUBS, 8, 256), F32),
            pltpu.VMEM((SUBS, 8, 128), F32),
            pltpu.VMEM((2 * SUBS, 256, 256), BF16),
        ],
        1 << 32,
        arrived,
        *fold_tables(),
    )
    returned = lax.all_to_all(values, "sub", split_axis=0, concat_axis=0, tiled=True)
    return call(
        unpack_kernel,
        jax.ShapeDtypeStruct((2, DEV_ROWS), F32),
        [vmem()] * 4,
        [pltpu.VMEM((SUBS, 8, 128), F32)],
        1 << 32,
        returned,
        owner_row,
        position,
        slots,
    )


def solution(mesh):
    placed = (
        P("facet", None, "sub", None),
        P(),
        P(),
        P(None, ("facet", "sub")),
        P(("facet", "sub"), None),
    )
    return jax.shard_map(
        per_device, mesh=mesh, in_specs=placed, out_specs=P(None, ("facet", "sub")), check_vma=False
    )
```

```python
import math

import jax
import jax.numpy as jnp
import ml_dtypes
import numpy as np
from jax import lax
from jax.experimental import pallas as pl
from jax.experimental.pallas import tpu as pltpu
from jax.sharding import PartitionSpec as P

N_IMG = 65536
XA = 256
ROWS = 64
SUBS = 32
CAP = 512
DEV_ROWS = 4096
PARTS = 16
F32 = jnp.float32
BF16 = jnp.bfloat16


def split_host(table):
    table = np.asarray(table, np.float32)
    high = table.astype(ml_dtypes.bfloat16)
    low = (table - high.astype(np.float32)).astype(ml_dtypes.bfloat16)
    return high, low


def transform_tables():
    turn = 2.0 * np.pi / 256.0
    a, q = np.arange(64), np.arange(256)
    first = np.outer(a, q) % 256 * turn
    real, imag = np.cos(first), -np.sin(first)
    outer = np.block([[real, imag], [-imag, real]])
    angle = np.outer(q, q) * (2.0 * np.pi / N_IMG)
    twiddle = np.stack([np.cos(angle), -np.sin(angle)]) / 128.0
    second = np.outer(q, q) % 256 * turn
    real, imag = np.cos(second), -np.sin(second)
    inner = np.stack([real, imag], axis=1).astype(np.float32)
    return inner, split_host(outer) + (twiddle.astype(np.float32),)


def fold_tables():
    order = [16 * h + 1 + j for j in range(16) for h in range(8)]
    cells = np.zeros((XA, 3 * 128), np.float32)
    for place, m in enumerate(order):
        if m < 128:
            cells[128 + m, place] += 1.0
            cells[128 + m, 128 + place] += 1.0
        cells[128 - m, place] += 1.0
        cells[128 - m, 128 + place] -= 1.0
    cells[128, 256:] = 1.0
    order = [4 * g + j for j in range(4) for g in range(8)]
    even, odd = np.zeros((2, 32, ROWS), np.float32)
    for place, k in enumerate(order):
        for row, sign in ((32 + k, 1.0), (31 - k, -1.0)):
            at = row % 2 * SUBS + row // 2
            even[place, at], odd[place, at] = 1.0, sign
    none = np.zeros_like(even)
    with_cos = np.block([[even, none], [none, odd], [none, even], [odd, none]])
    with_sin = np.block([[none, -even], [odd, none], [even, none], [none, -odd]])
    return [table.astype(ml_dtypes.bfloat16) for table in (cells, with_cos, with_sin)]


def turn_polynomials(reach, cos_terms, sin_terms):
    nodes = (np.cos(np.pi * (np.arange(400) + 0.5) / 400) + 1.0) / 2.0 * reach**2
    r = np.sqrt(nodes)
    fit = np.polynomial.chebyshev.Chebyshev.fit
    cosine = fit(nodes, np.cos(2 * np.pi * r), cos_terms - 1, domain=[0, reach**2])
    sine = fit(nodes, np.sin(2 * np.pi * r) / r, sin_terms - 1, domain=[0, reach**2])
    plain = np.polynomial.Polynomial
    return (
        [float(c) for c in cosine.convert(kind=plain).coef],
        [float(c) for c in sine.convert(kind=plain).coef],
    )


ANY_TURN = turn_polynomials(0.5, 7, 6)
QUARTER_TURN = turn_polynomials(0.25, 5, 5)
SMALL_TURN = turn_polynomials(0.125, 4, 4)


def reduced(turns):
    return turns - jnp.round(turns)


def unit_turns(r, terms):
    square = r * r
    cosine, sine = (jnp.full_like(square, part[-1]) for part in terms)
    for term in terms[0][-2::-1]:
        cosine = cosine * square + term
    for term in terms[1][-2::-1]:
        sine = sine * square + term
    return cosine, sine * r


def double_cos(half_step):
    return 2.0 - 4.0 * (half_step[1] * half_step[1])


def step_on(last, before, twice):
    return tuple(twice * x - y for x, y in zip(last, before))


def split_in_kernel(values):
    high = values.astype(BF16)
    return high, (values - high.astype(F32)).astype(BF16)


def iota(shape, axis):
    return lax.broadcasted_iota(jnp.int32, shape, axis)


def pack_kernel(
    starts_ref, coords_ref, owners_ref, inner_ref, packed_ref, position_ref, slots_ref, high_ref, low_ref, chosen
):
    for s in range(SUBS):
        run = starts_ref[s] // 256
        chosen[4 * s : 4 * s + 2, :] = inner_ref[run]
        chosen[4 * s + 2 : 4 * s + 4, :] = inner_ref[(run + 1) % 256]
    high_ref[...], low_ref[...] = split_in_kernel(chosen[...])
    width = 256
    blocks = DEV_ROWS // width
    owner_of = iota((SUBS, width), 0)
    slot_of = iota((CAP, width), 0)
    upper = (iota((width, width), 0) <= iota((width, width), 1)).astype(F32).astype(BF16)
    hots = []
    for block in range(blocks):
        match = owners_ref[:, pl.ds(block * width, width)] == owner_of
        hots.append(match.astype(F32))
    running = jnp.dot(
        jnp.concatenate(hots, axis=0).astype(BF16), upper, preferred_element_type=F32
    )
    carry = jnp.zeros((SUBS, 1), F32)
    positions = []
    for block in range(blocks):
        mine = running[SUBS * block : SUBS * block + SUBS]
        rank = jnp.sum(hots[block] * (mine + carry), axis=0, keepdims=True) - 1.0
        carry = carry + mine[:, width - 1 : width]
        positions.append(rank.astype(jnp.int32))
        lanes = pl.ds(block * width, width)
        position_ref[:, lanes] = positions[-1]
        own_slots = (iota((256, width), 0) == positions[-1] % 256).astype(F32)
        slots_ref[:, lanes] = own_slots.astype(BF16)
    total = jnp.zeros((4 * SUBS, CAP), F32)
    for block in range(blocks):
        lanes = pl.ds(block * width, width)
        slots = (slot_of == positions[block]).astype(F32).astype(BF16)
        rows = []
        for axis in range(2):
            for piece in split_in_kernel(coords_ref[axis : axis + 1, lanes]):
                rows.append((hots[block] * piece.astype(F32)).astype(BF16))
        total = total + lax.dot_general(
            jnp.concatenate(rows, axis=0),
            slots,
            (((1,), (1,)), ((), ())),
            preferred_element_type=F32,
        )
    for piece in range(4):
        for quarter in range(4):
            packed_ref[:, 4 * piece + quarter, :] = total[
                SUBS * piece : SUBS * piece + SUBS, 128 * quarter : 128 * quarter + 128
            ]


def split_dot(left_pair, right_pair):
    left_high, left_low = left_pair
    right_high, right_low = right_pair
    out = jnp.dot(left_high, right_high, preferred_element_type=F32)
    out = out + jnp.dot(left_low, right_high, preferred_element_type=F32)
    return out + jnp.dot(left_high, right_low, preferred_element_type=F32)


def spread_kernel(facets_ref, out_ref, rows):
    for part in range(2):
        for r in range(2):
            for block in range(16):
                at = 32 * part + 16 * r + block
                rows[at : at + 1, :] = facets_ref[
                    0, part, r : r + 1, 128 * block : 128 * block + 128
                ]
    for f in range(8):
        out_ref[f] = rows[...]


def window_kernel(
    starts_ref,
    image_ref,
    taper_ref,
    packed_ref,
    chosen_h,
    chosen_l,
    outer_h,
    outer_l,
    twiddle_ref,
    out_ref,
    columns,
    payload,
):
    payload[:, 8:24, :] = packed_ref[...]
    reals, imags = [], []
    for r in range(2):
        for part in range(2):
            for f in range(8):
                for side in range(2):
                    line = image_ref[f, pl.ds(32 * part + 16 * r + side, 8, stride=2), :]
                    at = 64 * part + 8 * f
                    columns[r, at : at + 8, 128 * side : 128 * side + 128] = (
                        line * taper_ref[pl.ds(side, 8, stride=2), :]
                    )
        mixed = split_dot(split_in_kernel(columns[r].T), (outer_h[...], outer_l[...]))
        real, imag = mixed[:, :256], mixed[:, 256:]
        turn_real, turn_imag = twiddle_ref[0], twiddle_ref[1]
        reals.append(real * turn_real - imag * turn_imag)
        imags.append(real * turn_imag + imag * turn_real)
    both = jnp.concatenate(reals + imags, axis=1)
    runs = split_dot((chosen_h[...], chosen_l[...]), split_in_kernel(both))
    lane = iota((2, 1024), 1) % 256
    for s in range(SUBS):
        low = starts_ref[s] % 256
        mine = runs[4 * s : 4 * s + 4]
        mine = jnp.where(lane >= low, mine[0:2], mine[2:4])
        real = mine[0:1, :512] - mine[1:2, 512:]
        imag = mine[1:2, :512] + mine[0:1, 512:]
        window = jnp.concatenate([real[:, :256], real[:, 256:], imag[:, :256], imag[:, 256:]], axis=0)
        window = pltpu.roll(window, (256 - low) % 256, 1)
        payload[s, 0:4, :] = window[:, :128]
        payload[s, 4:8, :] = window[:, 128:]
    out_ref[...] = payload[...].astype(BF16)


def degrid_kernel(
    arrived_ref, cells_ref, with_cos_ref, with_sin_ref, out_ref, arrived, coords, weights, bias, partial, values, phases
):
    arrived[...] = arrived_ref[...].astype(F32)
    grid = jnp.concatenate(
        [
            jnp.concatenate([arrived[:, 4 * side + plane, :] for plane in range(4)], axis=0)
            for side in range(2)
        ],
        axis=1,
    )
    for axis in range(2):
        for quarter in range(4):
            at = 8 + 8 * axis + quarter
            coords[axis, quarter] = arrived[:, at, :] + arrived[:, at + 4, :]
    by_cell = jnp.dot(grid.astype(BF16), cells_ref[...], preferred_element_type=F32)
    high, low = split_in_kernel(by_cell)

    def fold(matrix, columns):
        return jnp.dot(matrix, high[:, columns], preferred_element_type=F32) + jnp.dot(
            matrix, low[:, columns], preferred_element_type=F32
        )

    weights[:, 0:128] = fold(with_cos_ref[...], slice(0, 128)).astype(BF16)
    weights[:, 128:256] = fold(with_sin_ref[...], slice(128, 256)).astype(BF16)
    bias[...] = fold(with_cos_ref[...], slice(256, 384))

    step_row = iota((8, 256), 0).astype(F32)
    cell_scale = (16.0 * step_row + 8.0) * (1.0 / XA)
    row_scale = (4.0 * step_row + 2.0) * (1.0 / ROWS)
    def place(step, part):
        return (step * PARTS + part) // 2, part % 2

    def seeds(step, part, axis, scale):
        source, half = place(step, part)
        where = jnp.concatenate(
            [
                jnp.broadcast_to(
                    coords[axis, 2 * half + side, pl.ds(source, 1), :], (8, 128)
                )
                for side in range(2)
            ],
            axis=1,
        )
        return where, unit_turns(reduced(where * scale), ANY_TURN)

    def make_phases(step, part):
        u, below = seeds(step, part, 1, cell_scale)
        (a_cos, a_sin), (b_cos, b_sin) = below, unit_turns(u * (1.0 / XA), SMALL_TURN)
        above = (a_cos * b_cos - a_sin * b_sin, a_sin * b_cos + a_cos * b_sin)
        twice = b_cos + b_cos
        pieces = [[None] * 8, [None] * 8]
        for direction in (-1, 1):
            last, before, at = (below, above, 3) if direction < 0 else (above, below, 4)
            while True:
                following = step_on(last, before, twice)
                pair = (following, last) if direction < 0 else (last, following)
                for kind in range(2):
                    pieces[kind][at] = jnp.concatenate(
                        [pair[0][kind], pair[1][kind]], axis=0
                    ).astype(BF16)
                at += direction
                if not 0 <= at < 8:
                    break
                before, last = following, step_on(following, last, twice)
        return pieces[0] + pieces[1]

    def evaluate(step, part, inner):
        v, (a_cos, a_sin) = seeds(step, part, 0, row_scale)
        half_step = unit_turns(v * (0.5 / ROWS), QUARTER_TURN)
        b_cos, b_sin = half_step
        cc, ss = a_cos * b_cos, a_sin * b_sin
        sc, cs = a_sin * b_cos, a_cos * b_sin
        below, above, twice = (cc + ss, sc - cs), (cc - ss, sc + cs), double_cos(half_step)
        total_real = total_imag = 0.0
        for j in (1, 0, 2, 3):
            if j == 0:
                cosk, sink = step_on(below, above, twice)
            elif j == 3:
                cosk, sink = step_on(above, below, twice)
            else:
                cosk, sink = below if j == 1 else above
            mine = []
            for at in range(8 * j, 8 * j + 128, 32):
                constant = bias[at : at + 8, :]
                mine.append(inner[at : at + 8] + jnp.concatenate([constant, constant], axis=1))
            total_real += mine[0] * cosk - mine[1] * sink
            total_imag += mine[2] * cosk + mine[3] * sink
        return total_real, total_imag

    steps = 2 * SUBS // PARTS

    def fill(made, buffer):
        for number, piece in enumerate(made):
            buffer[16 * number : 16 * number + 16, :] = piece

    def produce(step, carry):
        for part in range(PARTS):
            fill(make_phases(step, part), phases.at[step * PARTS + part])
        return carry

    def consume(step, carry):
        for part in range(2 * PARTS):
            inner = jnp.dot(
                weights[...], phases[step * 2 * PARTS + part], preferred_element_type=F32
            )
            sums = evaluate(2 * step, part, inner)
            source, half = place(2 * step, part)
            for axis in range(2):
                partial[axis, half, source] = sums[axis]
        return carry

    lax.fori_loop(0, steps, produce, 0)
    lax.fori_loop(0, steps // 2, consume, 0)
    for half in range(2):
        where = jnp.concatenate([coords[0, 2 * half], coords[0, 2 * half + 1]], axis=1)
        back_cos, back_sin = unit_turns(where * (0.5 / ROWS), QUARTER_TURN)
        real_sum, imag_sum = (
            sum(partial[axis, half, :, i, :] for i in range(8)) * (1.0 / 128.0) for axis in range(2)
        )
        for axis, value in enumerate(
            (real_sum * back_cos + imag_sum * back_sin, imag_sum * back_cos - real_sum * back_sin)
        ):
            at = 4 * axis + 2 * half
            values[:, at, :] = value[:, :128]
            values[:, at + 1, :] = value[:, 128:]
    out_ref[...] = values[...].astype(BF16)


def unpack_kernel(returned_ref, owners_ref, position_ref, slots_ref, out_ref, values):
    values[...] = returned_ref[...].astype(F32)
    table = jnp.concatenate(
        [
            jnp.concatenate([values[:, at, :], values[:, at + 1, :]], axis=1)
            for at in range(0, 8, 2)
        ],
        axis=0,
    ).astype(BF16)
    width = 512
    owner_of = iota((2 * SUBS, width), 0) % SUBS
    late_of = iota((2 * SUBS, width), 0) // SUBS
    for block in range(DEV_ROWS // width):
        lanes = pl.ds(block * width, width)
        match = (owners_ref[:, lanes] == owner_of) & (position_ref[:, lanes] // 256 == late_of)
        picked = jnp.dot(table, slots_ref[:, lanes], preferred_element_type=F32)
        for axis in range(2):
            out_ref[axis : axis + 1, lanes] = jnp.sum(
                jnp.where(match, picked[64 * axis : 64 * axis + 64], 0.0), axis=0, keepdims=True
            )


def vmem():
    return pl.BlockSpec(memory_space=pltpu.VMEM)


def smem():
    return pl.BlockSpec(memory_space=pltpu.SMEM)


def call(kernel, out_shape, in_specs, scratch, flops, *operands):
    return pl.pallas_call(
        kernel,
        out_shape=out_shape,
        in_specs=in_specs,
        out_specs=jax.tree.map(lambda _: vmem(), out_shape),
        scratch_shapes=scratch,
        compiler_params=pltpu.CompilerParams(vmem_limit_bytes=40 * 1024 * 1024),
        cost_estimate=pl.CostEstimate(flops=flops, bytes_accessed=1 << 20, transcendentals=0),
    )(*operands)


def per_device(facets, taper_weight, offsets, point_coords, owners):
    facet_index = lax.axis_index("facet")
    image = call(
        spread_kernel,
        jax.ShapeDtypeStruct((8, 64, 128), F32),
        [vmem()],
        [pltpu.VMEM((64, 128), F32)],
        0,
        facets,
    )
    image = lax.all_to_all(image, "facet", split_axis=0, concat_axis=0, tiled=True)
    owner_row = owners.reshape(1, DEV_ROWS)
    starts = lax.dynamic_slice(offsets, (facet_index * SUBS,), (SUBS,))
    inner, tables = transform_tables()
    packed, position, slots, chosen_h, chosen_l = call(
        pack_kernel,
        (
            jax.ShapeDtypeStruct((SUBS, 16, 128), F32),
            jax.ShapeDtypeStruct((1, DEV_ROWS), jnp.int32),
            jax.ShapeDtypeStruct((256, DEV_ROWS), BF16),
            jax.ShapeDtypeStruct((128, 256), BF16),
            jax.ShapeDtypeStruct((128, 256), BF16),
        ),
        [smem()] + [vmem()] * 3,
        [pltpu.VMEM((128, 256), F32)],
        1 << 32,
        starts,
        point_coords,
        owner_row,
        inner,
    )
    payload = call(
        window_kernel,
        jax.ShapeDtypeStruct((SUBS, 24, 128), BF16),
        [smem()] + [vmem()] * 8,
        [pltpu.VMEM((2, 128, 256), F32), pltpu.VMEM((SUBS, 24, 128), F32)],
        1 << 32,
        starts,
        image,
        taper_weight.reshape(16, 128),
        packed,
        chosen_h,
        chosen_l,
        *tables,
    )
    arrived = lax.all_to_all(payload, "sub", split_axis=0, concat_axis=0, tiled=True)
    values = call(
        degrid_kernel,
        jax.ShapeDtypeStruct((SUBS, 8, 128), BF16),
        [vmem()] * 4,
        [
            pltpu.VMEM((SUBS, 24, 128), F32),
            pltpu.VMEM((2, 4, SUBS, 128), F32),
            pltpu.VMEM((128, 256), BF16),
            pltpu.VMEM((128, 128), F32),
            pltpu.VMEM((2, 2, SUBS, 8, 256), F32),
            pltpu.VMEM((SUBS, 8, 128), F32),
            pltpu.VMEM((2 * SUBS, 256, 256), BF16),
        ],
        1 << 32,
        arrived,
        *fold_tables(),
    )
    returned = lax.all_to_all(values, "sub", split_axis=0, concat_axis=0, tiled=True)
    return call(
        unpack_kernel,
        jax.ShapeDtypeStruct((2, DEV_ROWS), F32),
        [vmem()] * 4,
        [pltpu.VMEM((SUBS, 8, 128), F32)],
        1 << 32,
        returned,
        owner_row,
        position,
        slots,
    )


def solution(mesh):
    placed = (
        P("facet", None, "sub", None),
        P(),
        P(),
        P(None, ("facet", "sub")),
        P(("facet", "sub"), None),
    )
    return jax.shard_map(
        per_device, mesh=mesh, in_specs=placed, out_specs=P(None, ("facet", "sub")), check_vma=False
    )
```

```python
import math

import jax
import jax.numpy as jnp
import ml_dtypes
import numpy as np
from jax import lax
from jax.experimental import pallas as pl
from jax.experimental.pallas import tpu as pltpu
from jax.sharding import PartitionSpec as P

N_IMG = 65536
XA = 256
ROWS = 64
SUBS = 32
CAP = 512
DEV_ROWS = 4096
PARTS = 16
F32 = jnp.float32
BF16 = jnp.bfloat16


def split_host(table):
    table = np.asarray(table, np.float32)
    high = table.astype(ml_dtypes.bfloat16)
    low = (table - high.astype(np.float32)).astype(ml_dtypes.bfloat16)
    return high, low


def transform_tables():
    turn = 2.0 * np.pi / 256.0
    a, q = np.arange(64), np.arange(256)
    first = np.outer(a, q) % 256 * turn
    real, imag = np.cos(first), -np.sin(first)
    outer = np.block([[real, imag], [-imag, real]])
    angle = np.outer(q, q) * (2.0 * np.pi / N_IMG)
    twiddle = np.stack([np.cos(angle), -np.sin(angle)]) / 128.0
    second = np.outer(q, q) % 256 * turn
    real, imag = np.cos(second), -np.sin(second)
    inner = np.stack([real, imag], axis=1).astype(np.float32)
    return inner, split_host(outer) + (twiddle.astype(np.float32),)


def fold_tables():
    order = [16 * h + 1 + j for j in range(16) for h in range(8)]
    cells = np.zeros((XA, 3 * 128), np.float32)
    for place, m in enumerate(order):
        if m < 128:
            cells[128 + m, place] += 1.0
            cells[128 + m, 128 + place] += 1.0
        cells[128 - m, place] += 1.0
        cells[128 - m, 128 + place] -= 1.0
    cells[128, 256:] = 1.0
    order = [4 * g + j for j in range(4) for g in range(8)]
    even, odd = np.zeros((2, 32, ROWS), np.float32)
    for place, k in enumerate(order):
        for row, sign in ((32 + k, 1.0), (31 - k, -1.0)):
            at = row % 2 * SUBS + row // 2
            even[place, at], odd[place, at] = 1.0, sign
    none = np.zeros_like(even)
    with_cos = np.block([[even, none], [none, odd], [none, even], [odd, none]])
    with_sin = np.block([[none, -even], [odd, none], [even, none], [none, -odd]])
    return [table.astype(ml_dtypes.bfloat16) for table in (cells, with_cos, with_sin)]


def turn_polynomials(reach, cos_terms, sin_terms):
    nodes = (np.cos(np.pi * (np.arange(400) + 0.5) / 400) + 1.0) / 2.0 * reach**2
    r = np.sqrt(nodes)
    fit = np.polynomial.chebyshev.Chebyshev.fit
    cosine = fit(nodes, np.cos(2 * np.pi * r), cos_terms - 1, domain=[0, reach**2])
    sine = fit(nodes, np.sin(2 * np.pi * r) / r, sin_terms - 1, domain=[0, reach**2])
    plain = np.polynomial.Polynomial
    return (
        [float(c) for c in cosine.convert(kind=plain).coef],
        [float(c) for c in sine.convert(kind=plain).coef],
    )


ANY_TURN = turn_polynomials(0.5, 7, 6)
QUARTER_TURN = turn_polynomials(0.25, 5, 5)
SMALL_TURN = turn_polynomials(0.125, 4, 4)


def reduced(turns):
    return turns - jnp.round(turns)


def unit_turns(r, terms):
    square = r * r
    cosine, sine = (jnp.full_like(square, part[-1]) for part in terms)
    for term in terms[0][-2::-1]:
        cosine = cosine * square + term
    for term in terms[1][-2::-1]:
        sine = sine * square + term
    return cosine, sine * r


def double_cos(half_step):
    return 2.0 - 4.0 * (half_step[1] * half_step[1])


def step_on(last, before, twice):
    return tuple(twice * x - y for x, y in zip(last, before))


def split_in_kernel(values):
    high = values.astype(BF16)
    return high, (values - high.astype(F32)).astype(BF16)


def iota(shape, axis):
    return lax.broadcasted_iota(jnp.int32, shape, axis)


def window_start(offsets_ref, s):
    return offsets_ref[lax.axis_index("facet") * SUBS + s]


def pack_kernel(
    offsets_ref, coords_ref, owners_ref, inner_ref, packed_ref, position_ref, slots_ref, high_ref, low_ref, chosen
):
    for s in range(SUBS):
        run = window_start(offsets_ref, s) // 256
        chosen[4 * s : 4 * s + 2, :] = inner_ref[run]
        chosen[4 * s + 2 : 4 * s + 4, :] = inner_ref[(run + 1) % 256]
    high_ref[...], low_ref[...] = split_in_kernel(chosen[...])
    width = 256
    blocks = DEV_ROWS // width
    owner_of = iota((SUBS, width), 0)
    slot_of = iota((CAP, width), 0)
    upper = (iota((width, width), 0) <= iota((width, width), 1)).astype(F32).astype(BF16)
    hots = []
    for block in range(blocks):
        match = owners_ref[:, pl.ds(block * width, width)] == owner_of
        hots.append(match.astype(F32))
    running = jnp.dot(
        jnp.concatenate(hots, axis=0).astype(BF16), upper, preferred_element_type=F32
    )
    carry = jnp.zeros((SUBS, 1), F32)
    positions = []
    for block in range(blocks):
        mine = running[SUBS * block : SUBS * block + SUBS]
        rank = jnp.sum(hots[block] * (mine + carry), axis=0, keepdims=True) - 1.0
        carry = carry + mine[:, width - 1 : width]
        positions.append(rank.astype(jnp.int32))
        lanes = pl.ds(block * width, width)
        position_ref[:, lanes] = positions[-1]
        own_slots = (iota((256, width), 0) == positions[-1] % 256).astype(F32)
        slots_ref[:, lanes] = own_slots.astype(BF16)
    total = jnp.zeros((4 * SUBS, CAP), F32)
    for block in range(blocks):
        lanes = pl.ds(block * width, width)
        slots = (slot_of == positions[block]).astype(F32).astype(BF16)
        rows = []
        for axis in range(2):
            for piece in split_in_kernel(coords_ref[axis : axis + 1, lanes]):
                rows.append((hots[block] * piece.astype(F32)).astype(BF16))
        total = total + lax.dot_general(
            jnp.concatenate(rows, axis=0),
            slots,
            (((1,), (1,)), ((), ())),
            preferred_element_type=F32,
        )
    for piece in range(4):
        for quarter in range(4):
            packed_ref[:, 4 * piece + quarter, :] = total[
                SUBS * piece : SUBS * piece + SUBS, 128 * quarter : 128 * quarter + 128
            ]


def split_dot(left_pair, right_pair):
    left_high, left_low = left_pair
    right_high, right_low = right_pair
    out = jnp.dot(left_high, right_high, preferred_element_type=F32)
    out = out + jnp.dot(left_low, right_high, preferred_element_type=F32)
    return out + jnp.dot(left_high, right_low, preferred_element_type=F32)


def spread_kernel(facets_ref, out_ref, rows):
    for part in range(2):
        for r in range(2):
            for block in range(16):
                at = 32 * part + 16 * r + block
                rows[at : at + 1, :] = facets_ref[
                    0, part, r : r + 1, 128 * block : 128 * block + 128
                ]
    for f in range(8):
        out_ref[f] = rows[...]


def window_kernel(
    offsets_ref,
    image_ref,
    taper_ref,
    packed_ref,
    chosen_h,
    chosen_l,
    outer_h,
    outer_l,
    twiddle_ref,
    out_ref,
    columns,
    payload,
):
    payload[:, 8:24, :] = packed_ref[...]
    reals, imags = [], []
    for r in range(2):
        for part in range(2):
            for f in range(8):
                for side in range(2):
                    line = image_ref[f, pl.ds(32 * part + 16 * r + side, 8, stride=2), :]
                    at = 64 * part + 8 * f
                    columns[r, at : at + 8, 128 * side : 128 * side + 128] = (
                        line * taper_ref[pl.ds(side, 8, stride=2), :]
                    )
        mixed = split_dot(split_in_kernel(columns[r].T), (outer_h[...], outer_l[...]))
        real, imag = mixed[:, :256], mixed[:, 256:]
        turn_real, turn_imag = twiddle_ref[0], twiddle_ref[1]
        reals.append(real * turn_real - imag * turn_imag)
        imags.append(real * turn_imag + imag * turn_real)
    both = jnp.concatenate(reals + imags, axis=1)
    runs = split_dot((chosen_h[...], chosen_l[...]), split_in_kernel(both))
    lane = iota((2, 1024), 1) % 256
    for s in range(SUBS):
        low = window_start(offsets_ref, s) % 256
        mine = runs[4 * s : 4 * s + 4]
        mine = jnp.where(lane >= low, mine[0:2], mine[2:4])
        real = mine[0:1, :512] - mine[1:2, 512:]
        imag = mine[1:2, :512] + mine[0:1, 512:]
        window = jnp.concatenate([real[:, :256], real[:, 256:], imag[:, :256], imag[:, 256:]], axis=0)
        window = pltpu.roll(window, (256 - low) % 256, 1)
        payload[s, 0:4, :] = window[:, :128]
        payload[s, 4:8, :] = window[:, 128:]
    out_ref[...] = payload[...].astype(BF16)


def degrid_kernel(
    arrived_ref, cells_ref, with_cos_ref, with_sin_ref, out_ref, arrived, coords, weights, bias, partial, values, phases
):
    arrived[...] = arrived_ref[...].astype(F32)
    grid = jnp.concatenate(
        [
            jnp.concatenate([arrived[:, 4 * side + plane, :] for plane in range(4)], axis=0)
            for side in range(2)
        ],
        axis=1,
    )
    for axis in range(2):
        for quarter in range(4):
            at = 8 + 8 * axis + quarter
            coords[axis, quarter] = arrived[:, at, :] + arrived[:, at + 4, :]
    by_cell = jnp.dot(grid.astype(BF16), cells_ref[...], preferred_element_type=F32)
    high, low = split_in_kernel(by_cell)

    def fold(matrix, columns):
        return jnp.dot(matrix, high[:, columns], preferred_element_type=F32) + jnp.dot(
            matrix, low[:, columns], preferred_element_type=F32
        )

    weights[:, 0:128] = fold(with_cos_ref[...], slice(0, 128)).astype(BF16)
    weights[:, 128:256] = fold(with_sin_ref[...], slice(128, 256)).astype(BF16)
    bias[...] = fold(with_cos_ref[...], slice(256, 384))

    step_row = iota((8, 256), 0).astype(F32)
    cell_scale = (16.0 * step_row + 8.0) * (1.0 / XA)
    row_scale = (4.0 * step_row + 2.0) * (1.0 / ROWS)
    def place(step, part):
        return (step * PARTS + part) // 2, part % 2

    def seeds(step, part, axis, scale):
        source, half = place(step, part)
        where = jnp.concatenate(
            [
                jnp.broadcast_to(
                    coords[axis, 2 * half + side, pl.ds(source, 1), :], (8, 128)
                )
                for side in range(2)
            ],
            axis=1,
        )
        return where, unit_turns(reduced(where * scale), ANY_TURN)

    def make_phases(step, part):
        u, below = seeds(step, part, 1, cell_scale)
        (a_cos, a_sin), (b_cos, b_sin) = below, unit_turns(u * (1.0 / XA), SMALL_TURN)
        above = (a_cos * b_cos - a_sin * b_sin, a_sin * b_cos + a_cos * b_sin)
        twice = b_cos + b_cos
        pieces = [[None] * 8, [None] * 8]
        for direction in (-1, 1):
            last, before, at = (below, above, 3) if direction < 0 else (above, below, 4)
            while True:
                following = step_on(last, before, twice)
                pair = (following, last) if direction < 0 else (last, following)
                for kind in range(2):
                    pieces[kind][at] = jnp.concatenate(
                        [pair[0][kind], pair[1][kind]], axis=0
                    ).astype(BF16)
                at += direction
                if not 0 <= at < 8:
                    break
                before, last = following, step_on(following, last, twice)
        return pieces[0] + pieces[1]

    def evaluate(step, part, inner):
        v, (a_cos, a_sin) = seeds(step, part, 0, row_scale)
        half_step = unit_turns(v * (0.5 / ROWS), QUARTER_TURN)
        b_cos, b_sin = half_step
        cc, ss = a_cos * b_cos, a_sin * b_sin
        sc, cs = a_sin * b_cos, a_cos * b_sin
        below, above, twice = (cc + ss, sc - cs), (cc - ss, sc + cs), double_cos(half_step)
        total_real = total_imag = 0.0
        for j in (1, 0, 2, 3):
            if j == 0:
                cosk, sink = step_on(below, above, twice)
            elif j == 3:
                cosk, sink = step_on(above, below, twice)
            else:
                cosk, sink = below if j == 1 else above
            mine = []
            for at in range(8 * j, 8 * j + 128, 32):
                constant = bias[at : at + 8, :]
                mine.append(inner[at : at + 8] + jnp.concatenate([constant, constant], axis=1))
            total_real += mine[0] * cosk - mine[1] * sink
            total_imag += mine[2] * cosk + mine[3] * sink
        return total_real, total_imag

    steps = 2 * SUBS // PARTS

    def fill(made, buffer):
        for number, piece in enumerate(made):
            buffer[16 * number : 16 * number + 16, :] = piece

    def produce(step, carry):
        for part in range(PARTS):
            fill(make_phases(step, part), phases.at[step * PARTS + part])
        return carry

    def consume(step, carry):
        for part in range(2 * PARTS):
            inner = jnp.dot(
                weights[...], phases[step * 2 * PARTS + part], preferred_element_type=F32
            )
            sums = evaluate(2 * step, part, inner)
            source, half = place(2 * step, part)
            for axis in range(2):
                partial[axis, half, source] = sums[axis]
        return carry

    lax.fori_loop(0, steps, produce, 0)
    lax.fori_loop(0, steps // 2, consume, 0)
    for half in range(2):
        where = jnp.concatenate([coords[0, 2 * half], coords[0, 2 * half + 1]], axis=1)
        back_cos, back_sin = unit_turns(where * (0.5 / ROWS), QUARTER_TURN)
        real_sum, imag_sum = (
            sum(partial[axis, half, :, i, :] for i in range(8)) * (1.0 / 128.0) for axis in range(2)
        )
        for axis, value in enumerate(
            (real_sum * back_cos + imag_sum * back_sin, imag_sum * back_cos - real_sum * back_sin)
        ):
            at = 4 * axis + 2 * half
            values[:, at, :] = value[:, :128]
            values[:, at + 1, :] = value[:, 128:]
    out_ref[...] = values[...].astype(BF16)


def unpack_kernel(returned_ref, owners_ref, position_ref, slots_ref, out_ref, values):
    values[...] = returned_ref[...].astype(F32)
    table = jnp.concatenate(
        [
            jnp.concatenate([values[:, at, :], values[:, at + 1, :]], axis=1)
            for at in range(0, 8, 2)
        ],
        axis=0,
    ).astype(BF16)
    width = 512
    owner_of = iota((2 * SUBS, width), 0) % SUBS
    late_of = iota((2 * SUBS, width), 0) // SUBS
    for block in range(DEV_ROWS // width):
        lanes = pl.ds(block * width, width)
        match = (owners_ref[:, lanes] == owner_of) & (position_ref[:, lanes] // 256 == late_of)
        picked = jnp.dot(table, slots_ref[:, lanes], preferred_element_type=F32)
        for axis in range(2):
            out_ref[axis : axis + 1, lanes] = jnp.sum(
                jnp.where(match, picked[64 * axis : 64 * axis + 64], 0.0), axis=0, keepdims=True
            )


def vmem():
    return pl.BlockSpec(memory_space=pltpu.VMEM)


def smem():
    return pl.BlockSpec(memory_space=pltpu.SMEM)


def call(kernel, out_shape, in_specs, scratch, flops, *operands):
    return pl.pallas_call(
        kernel,
        out_shape=out_shape,
        in_specs=in_specs,
        out_specs=jax.tree.map(lambda _: vmem(), out_shape),
        scratch_shapes=scratch,
        compiler_params=pltpu.CompilerParams(vmem_limit_bytes=40 * 1024 * 1024),
        cost_estimate=pl.CostEstimate(flops=flops, bytes_accessed=1 << 20, transcendentals=0),
    )(*operands)


def per_device(facets, taper_weight, offsets, point_coords, owners):
    image = call(
        spread_kernel,
        jax.ShapeDtypeStruct((8, 64, 128), F32),
        [vmem()],
        [pltpu.VMEM((64, 128), F32)],
        0,
        facets,
    )
    image = lax.all_to_all(image, "facet", split_axis=0, concat_axis=0, tiled=True)
    owner_row = owners.reshape(1, DEV_ROWS)
    inner, tables = transform_tables()
    packed, position, slots, chosen_h, chosen_l = call(
        pack_kernel,
        (
            jax.ShapeDtypeStruct((SUBS, 16, 128), F32),
            jax.ShapeDtypeStruct((1, DEV_ROWS), jnp.int32),
            jax.ShapeDtypeStruct((256, DEV_ROWS), BF16),
            jax.ShapeDtypeStruct((128, 256), BF16),
            jax.ShapeDtypeStruct((128, 256), BF16),
        ),
        [smem()] + [vmem()] * 3,
        [pltpu.VMEM((128, 256), F32)],
        1 << 32,
        offsets,
        point_coords,
        owner_row,
        inner,
    )
    payload = call(
        window_kernel,
        jax.ShapeDtypeStruct((SUBS, 24, 128), BF16),
        [smem()] + [vmem()] * 8,
        [pltpu.VMEM((2, 128, 256), F32), pltpu.VMEM((SUBS, 24, 128), F32)],
        1 << 32,
        offsets,
        image,
        taper_weight.reshape(16, 128),
        packed,
        chosen_h,
        chosen_l,
        *tables,
    )
    arrived = lax.all_to_all(payload, "sub", split_axis=0, concat_axis=0, tiled=True)
    values = call(
        degrid_kernel,
        jax.ShapeDtypeStruct((SUBS, 8, 128), BF16),
        [vmem()] * 4,
        [
            pltpu.VMEM((SUBS, 24, 128), F32),
            pltpu.VMEM((2, 4, SUBS, 128), F32),
            pltpu.VMEM((128, 256), BF16),
            pltpu.VMEM((128, 128), F32),
            pltpu.VMEM((2, 2, SUBS, 8, 256), F32),
            pltpu.VMEM((SUBS, 8, 128), F32),
            pltpu.VMEM((2 * SUBS, 256, 256), BF16),
        ],
        1 << 32,
        arrived,
        *fold_tables(),
    )
    returned = lax.all_to_all(values, "sub", split_axis=0, concat_axis=0, tiled=True)
    return call(
        unpack_kernel,
        jax.ShapeDtypeStruct((2, DEV_ROWS), F32),
        [vmem()] * 4,
        [pltpu.VMEM((SUBS, 8, 128), F32)],
        1 << 32,
        returned,
        owner_row,
        position,
        slots,
    )


def solution(mesh):
    placed = (
        P("facet", None, "sub", None),
        P(),
        P(),
        P(None, ("facet", "sub")),
        P(("facet", "sub"), None),
    )
    return jax.shard_map(
        per_device, mesh=mesh, in_specs=placed, out_specs=P(None, ("facet", "sub")), check_vma=False
    )
```

```python
import math

import jax
import jax.numpy as jnp
import ml_dtypes
import numpy as np
from jax import lax
from jax.experimental import pallas as pl
from jax.experimental.pallas import tpu as pltpu
from jax.sharding import PartitionSpec as P

N_IMG = 65536
XA = 256
ROWS = 64
SUBS = 32
CAP = 512
DEV_ROWS = 4096
PARTS = 16
F32 = jnp.float32
BF16 = jnp.bfloat16


def split_host(table):
    table = np.asarray(table, np.float32)
    high = table.astype(ml_dtypes.bfloat16)
    low = (table - high.astype(np.float32)).astype(ml_dtypes.bfloat16)
    return high, low


def transform_tables():
    turn = 2.0 * np.pi / 256.0
    a, q = np.arange(64), np.arange(256)
    first = np.outer(a, q) % 256 * turn
    real, imag = np.cos(first), -np.sin(first)
    outer = np.block([[real, imag], [-imag, real]])
    angle = np.outer(q, q) * (2.0 * np.pi / N_IMG)
    twiddle = np.stack([np.cos(angle), -np.sin(angle)]) / 128.0
    second = np.outer(q, q) % 256 * turn
    real, imag = np.cos(second), -np.sin(second)
    inner = np.stack([real, imag], axis=1).astype(np.float32)
    return inner, split_host(outer) + (twiddle.astype(np.float32),)


def fold_tables():
    order = [16 * h + 1 + j for j in range(16) for h in range(8)]
    cells = np.zeros((XA, 3 * 128), np.float32)
    for place, m in enumerate(order):
        if m < 128:
            cells[128 + m, place] += 1.0
            cells[128 + m, 128 + place] += 1.0
        cells[128 - m, place] += 1.0
        cells[128 - m, 128 + place] -= 1.0
    cells[128, 256:] = 1.0
    order = [4 * g + j for j in range(4) for g in range(8)]
    even, odd = np.zeros((2, 32, ROWS), np.float32)
    for place, k in enumerate(order):
        for row, sign in ((32 + k, 1.0), (31 - k, -1.0)):
            at = row % 2 * SUBS + row // 2
            even[place, at], odd[place, at] = 1.0, sign
    none = np.zeros_like(even)
    with_cos = np.block([[even, none], [none, odd], [none, even], [odd, none]])
    with_sin = np.block([[none, -even], [odd, none], [even, none], [none, -odd]])
    return [table.astype(ml_dtypes.bfloat16) for table in (cells, with_cos, with_sin)]


def turn_polynomials(reach, cos_terms, sin_terms):
    nodes = (np.cos(np.pi * (np.arange(400) + 0.5) / 400) + 1.0) / 2.0 * reach**2
    r = np.sqrt(nodes)
    fit = np.polynomial.chebyshev.Chebyshev.fit
    cosine = fit(nodes, np.cos(2 * np.pi * r), cos_terms - 1, domain=[0, reach**2])
    sine = fit(nodes, np.sin(2 * np.pi * r) / r, sin_terms - 1, domain=[0, reach**2])
    plain = np.polynomial.Polynomial
    return (
        [float(c) for c in cosine.convert(kind=plain).coef],
        [float(c) for c in sine.convert(kind=plain).coef],
    )


ANY_TURN = turn_polynomials(0.5, 7, 6)
QUARTER_TURN = turn_polynomials(0.25, 5, 5)
SMALL_TURN = turn_polynomials(0.125, 4, 4)


def reduced(turns):
    return turns - jnp.round(turns)


def unit_turns(r, terms):
    square = r * r
    cosine, sine = (jnp.full_like(square, part[-1]) for part in terms)
    for term in terms[0][-2::-1]:
        cosine = cosine * square + term
    for term in terms[1][-2::-1]:
        sine = sine * square + term
    return cosine, sine * r


def double_cos(half_step):
    return 2.0 - 4.0 * (half_step[1] * half_step[1])


def step_on(last, before, twice):
    return tuple(twice * x - y for x, y in zip(last, before))


def split_in_kernel(values):
    high = values.astype(BF16)
    return high, (values - high.astype(F32)).astype(BF16)


def iota(shape, axis):
    return lax.broadcasted_iota(jnp.int32, shape, axis)


def window_start(offsets_ref, s):
    return offsets_ref[lax.axis_index("facet") * SUBS + s]


def pack_kernel(
    offsets_ref, coords_ref, owners_ref, inner_ref, packed_ref, position_ref, slots_ref, high_ref, low_ref, chosen
):
    for s in range(SUBS):
        run = window_start(offsets_ref, s) // 256
        chosen[4 * s : 4 * s + 2, :] = inner_ref[run]
        chosen[4 * s + 2 : 4 * s + 4, :] = inner_ref[(run + 1) % 256]
    high_ref[...], low_ref[...] = split_in_kernel(chosen[...])
    width = 256
    blocks = DEV_ROWS // width
    owner_of = iota((SUBS, width), 0)
    slot_of = iota((CAP, width), 0)
    upper = (iota((width, width), 0) <= iota((width, width), 1)).astype(F32).astype(BF16)
    hots = []
    for block in range(blocks):
        match = owners_ref[:, pl.ds(block * width, width)] == owner_of
        hots.append(match.astype(F32))
    running = jnp.dot(
        jnp.concatenate(hots, axis=0).astype(BF16), upper, preferred_element_type=F32
    )
    carry = jnp.zeros((SUBS, 1), F32)
    positions = []
    for block in range(blocks):
        mine = running[SUBS * block : SUBS * block + SUBS]
        rank = jnp.sum(hots[block] * (mine + carry), axis=0, keepdims=True) - 1.0
        carry = carry + mine[:, width - 1 : width]
        positions.append(rank.astype(jnp.int32))
        lanes = pl.ds(block * width, width)
        position_ref[:, lanes] = positions[-1]
        own_slots = (iota((256, width), 0) == positions[-1] % 256).astype(F32)
        slots_ref[:, lanes] = own_slots.astype(BF16)
    total = jnp.zeros((4 * SUBS, CAP), F32)
    for block in range(blocks):
        lanes = pl.ds(block * width, width)
        slots = (slot_of == positions[block]).astype(F32).astype(BF16)
        rows = []
        for axis in range(2):
            for piece in split_in_kernel(coords_ref[axis : axis + 1, lanes]):
                rows.append((hots[block] * piece.astype(F32)).astype(BF16))
        total = total + lax.dot_general(
            jnp.concatenate(rows, axis=0),
            slots,
            (((1,), (1,)), ((), ())),
            preferred_element_type=F32,
        )
    for piece in range(4):
        for quarter in range(4):
            packed_ref[:, 4 * piece + quarter, :] = total[
                SUBS * piece : SUBS * piece + SUBS, 128 * quarter : 128 * quarter + 128
            ]


def split_dot(left_pair, right_pair):
    left_high, left_low = left_pair
    right_high, right_low = right_pair
    out = jnp.dot(left_high, right_high, preferred_element_type=F32)
    out = out + jnp.dot(left_low, right_high, preferred_element_type=F32)
    return out + jnp.dot(left_high, right_low, preferred_element_type=F32)


def spread_kernel(facets_ref, out_ref, rows):
    for part in range(2):
        for r in range(2):
            for block in range(16):
                at = 32 * part + 16 * r + block
                rows[at : at + 1, :] = facets_ref[
                    0, part, r : r + 1, 128 * block : 128 * block + 128
                ]
    for f in range(8):
        out_ref[f] = rows[...]


def window_kernel(
    offsets_ref,
    image_ref,
    taper_ref,
    packed_ref,
    chosen_h,
    chosen_l,
    outer_h,
    outer_l,
    twiddle_ref,
    out_ref,
    columns,
    payload,
):
    payload[:, 8:24, :] = packed_ref[...]
    reals, imags = [], []
    for r in range(2):
        for part in range(2):
            for f in range(8):
                for side in range(2):
                    line = image_ref[f, pl.ds(32 * part + 16 * r + side, 8, stride=2), :]
                    at = 64 * part + 8 * f
                    columns[r, at : at + 8, 128 * side : 128 * side + 128] = (
                        line * taper_ref[pl.ds(side, 8, stride=2), :]
                    )
    by_column = jnp.concatenate([columns[0].T, columns[1].T], axis=0)
    mixed = split_dot(split_in_kernel(by_column), (outer_h[...], outer_l[...]))
    turn_real, turn_imag = twiddle_ref[0], twiddle_ref[1]
    for r in range(2):
        real, imag = mixed[256 * r : 256 * r + 256, :256], mixed[256 * r : 256 * r + 256, 256:]
        reals.append(real * turn_real - imag * turn_imag)
        imags.append(real * turn_imag + imag * turn_real)
    both = jnp.concatenate(reals + imags, axis=1)
    runs = split_dot((chosen_h[...], chosen_l[...]), split_in_kernel(both))
    lane = iota((2, 1024), 1) % 256
    for s in range(SUBS):
        low = window_start(offsets_ref, s) % 256
        mine = runs[4 * s : 4 * s + 4]
        mine = jnp.where(lane >= low, mine[0:2], mine[2:4])
        real = mine[0:1, :512] - mine[1:2, 512:]
        imag = mine[1:2, :512] + mine[0:1, 512:]
        window = jnp.concatenate([real[:, :256], real[:, 256:], imag[:, :256], imag[:, 256:]], axis=0)
        window = pltpu.roll(window, (256 - low) % 256, 1)
        payload[s, 0:4, :] = window[:, :128]
        payload[s, 4:8, :] = window[:, 128:]
    out_ref[...] = payload[...].astype(BF16)


def degrid_kernel(
    arrived_ref, cells_ref, with_cos_ref, with_sin_ref, out_ref, arrived, coords, weights, bias, partial, values, phases
):
    arrived[...] = arrived_ref[...].astype(F32)
    grid = jnp.concatenate(
        [
            jnp.concatenate([arrived[:, 4 * side + plane, :] for plane in range(4)], axis=0)
            for side in range(2)
        ],
        axis=1,
    )
    for axis in range(2):
        for quarter in range(4):
            at = 8 + 8 * axis + quarter
            coords[axis, quarter] = arrived[:, at, :] + arrived[:, at + 4, :]
    by_cell = jnp.dot(grid.astype(BF16), cells_ref[...], preferred_element_type=F32)
    high, low = split_in_kernel(by_cell)

    def fold(matrix, columns):
        return jnp.dot(matrix, high[:, columns], preferred_element_type=F32) + jnp.dot(
            matrix, low[:, columns], preferred_element_type=F32
        )

    weights[:, 0:128] = fold(with_cos_ref[...], slice(0, 128)).astype(BF16)
    weights[:, 128:256] = fold(with_sin_ref[...], slice(128, 256)).astype(BF16)
    bias[...] = fold(with_cos_ref[...], slice(256, 384))

    step_row = iota((8, 256), 0).astype(F32)
    cell_scale = (16.0 * step_row + 8.0) * (1.0 / XA)
    row_scale = (4.0 * step_row + 2.0) * (1.0 / ROWS)
    def place(step, part):
        return (step * PARTS + part) // 2, part % 2

    def seeds(step, part, axis, scale):
        source, half = place(step, part)
        where = jnp.concatenate(
            [
                jnp.broadcast_to(
                    coords[axis, 2 * half + side, pl.ds(source, 1), :], (8, 128)
                )
                for side in range(2)
            ],
            axis=1,
        )
        return where, unit_turns(reduced(where * scale), ANY_TURN)

    def make_phases(step, part):
        u, below = seeds(step, part, 1, cell_scale)
        (a_cos, a_sin), (b_cos, b_sin) = below, unit_turns(u * (1.0 / XA), SMALL_TURN)
        above = (a_cos * b_cos - a_sin * b_sin, a_sin * b_cos + a_cos * b_sin)
        twice = b_cos + b_cos
        pieces = [[None] * 8, [None] * 8]
        for direction in (-1, 1):
            last, before, at = (below, above, 3) if direction < 0 else (above, below, 4)
            while True:
                following = step_on(last, before, twice)
                pair = (following, last) if direction < 0 else (last, following)
                for kind in range(2):
                    pieces[kind][at] = jnp.concatenate(
                        [pair[0][kind], pair[1][kind]], axis=0
                    ).astype(BF16)
                at += direction
                if not 0 <= at < 8:
                    break
                before, last = following, step_on(following, last, twice)
        return pieces[0] + pieces[1]

    def evaluate(step, part, inner):
        v, (a_cos, a_sin) = seeds(step, part, 0, row_scale)
        half_step = unit_turns(v * (0.5 / ROWS), QUARTER_TURN)
        b_cos, b_sin = half_step
        cc, ss = a_cos * b_cos, a_sin * b_sin
        sc, cs = a_sin * b_cos, a_cos * b_sin
        below, above, twice = (cc + ss, sc - cs), (cc - ss, sc + cs), double_cos(half_step)
        total_real = total_imag = 0.0
        for j in (1, 0, 2, 3):
            if j == 0:
                cosk, sink = step_on(below, above, twice)
            elif j == 3:
                cosk, sink = step_on(above, below, twice)
            else:
                cosk, sink = below if j == 1 else above
            mine = []
            for at in range(8 * j, 8 * j + 128, 32):
                constant = bias[at : at + 8, :]
                mine.append(inner[at : at + 8] + jnp.concatenate([constant, constant], axis=1))
            total_real += mine[0] * cosk - mine[1] * sink
            total_imag += mine[2] * cosk + mine[3] * sink
        return total_real, total_imag

    steps = 2 * SUBS // PARTS

    def fill(made, buffer):
        for number, piece in enumerate(made):
            buffer[16 * number : 16 * number + 16, :] = piece

    def produce(step, carry):
        for part in range(PARTS):
            fill(make_phases(step, part), phases.at[step * PARTS + part])
        return carry

    def consume(step, carry):
        for part in range(2 * PARTS):
            inner = jnp.dot(
                weights[...], phases[step * 2 * PARTS + part], preferred_element_type=F32
            )
            sums = evaluate(2 * step, part, inner)
            source, half = place(2 * step, part)
            for axis in range(2):
                partial[axis, half, source] = sums[axis]
        return carry

    lax.fori_loop(0, steps, produce, 0)
    lax.fori_loop(0, steps // 2, consume, 0)
    for half in range(2):
        where = jnp.concatenate([coords[0, 2 * half], coords[0, 2 * half + 1]], axis=1)
        back_cos, back_sin = unit_turns(where * (0.5 / ROWS), QUARTER_TURN)
        real_sum, imag_sum = (
            sum(partial[axis, half, :, i, :] for i in range(8)) * (1.0 / 128.0) for axis in range(2)
        )
        for axis, value in enumerate(
            (real_sum * back_cos + imag_sum * back_sin, imag_sum * back_cos - real_sum * back_sin)
        ):
            at = 4 * axis + 2 * half
            values[:, at, :] = value[:, :128]
            values[:, at + 1, :] = value[:, 128:]
    out_ref[...] = values[...].astype(BF16)


def unpack_kernel(returned_ref, owners_ref, position_ref, slots_ref, out_ref, values):
    values[...] = returned_ref[...].astype(F32)
    table = jnp.concatenate(
        [
            jnp.concatenate([values[:, at, :], values[:, at + 1, :]], axis=1)
            for at in range(0, 8, 2)
        ],
        axis=0,
    ).astype(BF16)
    width = 512
    owner_of = iota((2 * SUBS, width), 0) % SUBS
    late_of = iota((2 * SUBS, width), 0) // SUBS
    for block in range(DEV_ROWS // width):
        lanes = pl.ds(block * width, width)
        match = (owners_ref[:, lanes] == owner_of) & (position_ref[:, lanes] // 256 == late_of)
        picked = jnp.dot(table, slots_ref[:, lanes], preferred_element_type=F32)
        for axis in range(2):
            out_ref[axis : axis + 1, lanes] = jnp.sum(
                jnp.where(match, picked[64 * axis : 64 * axis + 64], 0.0), axis=0, keepdims=True
            )


def vmem():
    return pl.BlockSpec(memory_space=pltpu.VMEM)


def smem():
    return pl.BlockSpec(memory_space=pltpu.SMEM)


def call(kernel, out_shape, in_specs, scratch, flops, *operands):
    return pl.pallas_call(
        kernel,
        out_shape=out_shape,
        in_specs=in_specs,
        out_specs=jax.tree.map(lambda _: vmem(), out_shape),
        scratch_shapes=scratch,
        compiler_params=pltpu.CompilerParams(vmem_limit_bytes=40 * 1024 * 1024),
        cost_estimate=pl.CostEstimate(flops=flops, bytes_accessed=1 << 20, transcendentals=0),
    )(*operands)


def per_device(facets, taper_weight, offsets, point_coords, owners):
    image = call(
        spread_kernel,
        jax.ShapeDtypeStruct((8, 64, 128), F32),
        [vmem()],
        [pltpu.VMEM((64, 128), F32)],
        0,
        facets,
    )
    image = lax.all_to_all(image, "facet", split_axis=0, concat_axis=0, tiled=True)
    owner_row = owners.reshape(1, DEV_ROWS)
    inner, tables = transform_tables()
    packed, position, slots, chosen_h, chosen_l = call(
        pack_kernel,
        (
            jax.ShapeDtypeStruct((SUBS, 16, 128), F32),
            jax.ShapeDtypeStruct((1, DEV_ROWS), jnp.int32),
            jax.ShapeDtypeStruct((256, DEV_ROWS), BF16),
            jax.ShapeDtypeStruct((128, 256), BF16),
            jax.ShapeDtypeStruct((128, 256), BF16),
        ),
        [smem()] + [vmem()] * 3,
        [pltpu.VMEM((128, 256), F32)],
        1 << 32,
        offsets,
        point_coords,
        owner_row,
        inner,
    )
    payload = call(
        window_kernel,
        jax.ShapeDtypeStruct((SUBS, 24, 128), BF16),
        [smem()] + [vmem()] * 8,
        [pltpu.VMEM((2, 128, 256), F32), pltpu.VMEM((SUBS, 24, 128), F32)],
        1 << 32,
        offsets,
        image,
        taper_weight.reshape(16, 128),
        packed,
        chosen_h,
        chosen_l,
        *tables,
    )
    arrived = lax.all_to_all(payload, "sub", split_axis=0, concat_axis=0, tiled=True)
    values = call(
        degrid_kernel,
        jax.ShapeDtypeStruct((SUBS, 8, 128), BF16),
        [vmem()] * 4,
        [
            pltpu.VMEM((SUBS, 24, 128), F32),
            pltpu.VMEM((2, 4, SUBS, 128), F32),
            pltpu.VMEM((128, 256), BF16),
            pltpu.VMEM((128, 128), F32),
            pltpu.VMEM((2, 2, SUBS, 8, 256), F32),
            pltpu.VMEM((SUBS, 8, 128), F32),
            pltpu.VMEM((2 * SUBS, 256, 256), BF16),
        ],
        1 << 32,
        arrived,
        *fold_tables(),
    )
    returned = lax.all_to_all(values, "sub", split_axis=0, concat_axis=0, tiled=True)
    return call(
        unpack_kernel,
        jax.ShapeDtypeStruct((2, DEV_ROWS), F32),
        [vmem()] * 4,
        [pltpu.VMEM((SUBS, 8, 128), F32)],
        1 << 32,
        returned,
        owner_row,
        position,
        slots,
    )


def solution(mesh):
    placed = (
        P("facet", None, "sub", None),
        P(),
        P(),
        P(None, ("facet", "sub")),
        P(("facet", "sub"), None),
    )
    return jax.shard_map(
        per_device, mesh=mesh, in_specs=placed, out_specs=P(None, ("facet", "sub")), check_vma=False
    )
```
